32 devices in a mesh: step: 2 (over x), frame: 4 (over y, core), strip: 4 (over z).
Axes of the slice: x: 2, y: 2, z: 4, core: 2. Of those that a mesh axis runs over, the one named last changes fastest.
Arguments:
- enc_feats: bfloat16 [320, 8, 32, 128], P('step', 'frame', 'strip'), may hold values from -64 to 64
- skip_feats: bfloat16 [320, 8, 32, 128], P('step', 'frame', 'strip'), may hold values from -64 to 64
- timesteps: int32 [2], P('step'), may hold values from 0 to 999
- time_first: bfloat16 [320, 1280], replicated, may hold values from -0.3125 to 0.3125
- time_second: bfloat16 [1280, 1280], replicated, may hold values from -0.15625 to 0.15625
- embed_proj: bfloat16 [1280, 320], replicated, may hold values from -0.15625 to 0.15625
- conv_first: bfloat16 [3, 3, 320, 640], replicated, may hold values from -0.078125 to 0.078125
- conv_second: bfloat16 [3, 3, 320, 320], replicated, may hold values from -0.109375 to 0.109375
- temporal_weight: bfloat16 [3, 320, 320], replicated, may hold values from -0.1875 to 0.1875
- skip_weight: bfloat16 [320, 640], replicated, may hold values from -0.25 to 0.25
Outputs:
- decoded: bfloat16 [2, 320, 8, 32, 128], P('step', None, 'frame', 'strip')
The draws below stay inside these ranges and needn't reach their ends.
All inputs are finite; a program needn't handle non-finite values.
Results may differ from the reference program's by a relative error of at most 0.0035.
Values may be sent and summed in bfloat16 or wider, within the bound.
A program may use at most 64 MiB of HBM per device.

```python
import math
import jax
import jax.numpy as jnp
from jax import lax

C = 320
GROUPS = 32
COLS = 128
TEMB = 1280
STEPS = 2
FRAMES = 8
ROWS = 32


def feature_field(key, salt):
    key = jax.random.fold_in(key, salt)
    key_chan, key_rough, key_main = jax.random.split(key, 3)
    frame_pos = jnp.arange(FRAMES, dtype=jnp.float32) / max(FRAMES - 1, 1)
    row_pos = jnp.arange(ROWS, dtype=jnp.float32) / max(ROWS - 1, 1)
    chan_pos = jax.random.uniform(key_chan, (C,), jnp.float32)
    rough_rows = jnp.exp(jax.random.uniform(key_rough, (FRAMES, ROWS), jnp.float32, math.log(0.6), math.log(1.6)))
    level_rows = 0.5 * (frame_pos[:, None] + row_pos[None, :])
    scale_field = jnp.exp(math.log(10.0) * (level_rows[None, :, :] + chan_pos[:, None, None] - 1.0)) * rough_rows[None, :, :]
    noise_field = jax.random.normal(key_main, (C, FRAMES, ROWS, COLS), jnp.float32)
    noise_field = jnp.clip(noise_field, -4.0, 4.0)
    return (scale_field[:, :, :, None] * noise_field).astype(jnp.bfloat16)


def draw_enc_feats(key, part):
    return feature_field(key, 11)


def draw_skip_feats(key, part):
    return feature_field(key, 23)


def normal_values(key, dims, scale, most, held_as=jnp.bfloat16):
    values = jax.random.normal(key, dims, jnp.float32) * scale
    return jnp.minimum(jnp.maximum(values, -most), most).astype(held_as)


def setup_inputs(seed: int = 0) -> dict:
    seeds = jax.random.split(jax.random.key(seed), 11)
    enc_feats = draw_enc_feats(jax.random.fold_in(seeds[10], 71), 0)
    skip_feats = draw_skip_feats(jax.random.fold_in(seeds[10], 71), 0)
    timesteps = jax.random.randint(seeds[2], (STEPS,), 0, 1000).astype(jnp.int32)
    time_first = normal_values(seeds[3], (C, TEMB), C ** -0.5, 0.3125)
    time_second = normal_values(seeds[4], (TEMB, TEMB), TEMB ** -0.5, 0.15625)
    embed_proj = normal_values(seeds[5], (TEMB, C), TEMB ** -0.5, 0.15625)
    conv_first = normal_values(seeds[6], (3, 3, C, 2 * C), (18 * C) ** -0.5, 0.078125)
    conv_second = normal_values(seeds[7], (3, 3, C, C), (9 * C) ** -0.5, 0.109375)
    temporal_weight = normal_values(seeds[8], (3, C, C), (3 * C) ** -0.5, 0.1875)
    skip_weight = normal_values(seeds[9], (C, 2 * C), (2 * C) ** -0.5, 0.25)
    return dict(enc_feats=enc_feats, skip_feats=skip_feats, timesteps=timesteps, time_first=time_first, time_second=time_second, embed_proj=embed_proj, conv_first=conv_first, conv_second=conv_second, temporal_weight=temporal_weight, skip_weight=skip_weight)


norm_eps = 1e-05

def conv_taps(padded, weights):
    row_count = padded.shape[2] - 2
    col_count = padded.shape[3]
    padded_cols = jnp.pad(padded.astype(jnp.float32), ((0, 0), (0, 0), (0, 0), (1, 1)))
    running = jnp.zeros((weights.shape[2], padded.shape[1], row_count, col_count), jnp.float32)
    for row_off in range(3):
        for col_off in range(3):
            tap_weight = weights[row_off, col_off].astype(jnp.float32)
            window = padded_cols[:, :, row_off:row_off + row_count, col_off:col_off + col_count]
            running = running + jnp.einsum('oi,ifhw->ofhw', tap_weight, window)
    return running

def group_silu(values, groups):
    per_group = values.shape[0] // groups
    count_all = values.shape[1] * values.shape[2] * values.shape[3] * per_group
    sum_one = lax.optimization_barrier(jnp.sum(values, axis=(1, 2, 3)))
    sum_two = lax.optimization_barrier(jnp.sum(values * values, axis=(1, 2, 3)))
    mean_group = sum_one.reshape(groups, per_group).sum(axis=1) / count_all
    square_group = sum_two.reshape(groups, per_group).sum(axis=1) / count_all
    rstd_group = lax.rsqrt(square_group - mean_group * mean_group + norm_eps)
    mean_chan = jnp.repeat(mean_group, per_group)
    rstd_chan = jnp.repeat(rstd_group, per_group)
    return jax.nn.silu((values - mean_chan[:, None, None, None]) * rstd_chan[:, None, None, None])

def reference(enc_feats, skip_feats, timesteps, time_first, time_second, embed_proj, conv_first, conv_second, temporal_weight, skip_weight):
    joined = jnp.concatenate([enc_feats, skip_feats], axis=0)
    act_in = group_silu(joined.astype(jnp.float32), GROUPS).astype(jnp.bfloat16)
    conv_out = conv_taps(jnp.pad(act_in, ((0, 0), (0, 0), (1, 1), (0, 0))), conv_first)
    skip_out = jnp.einsum('oi,ifhw->ofhw', skip_weight.astype(jnp.float32), joined.astype(jnp.float32))
    half_chans = C // 2
    freq_table = jnp.exp(-math.log(10000.0) * jnp.arange(half_chans, dtype=jnp.float32) / half_chans)
    angle_rows = timesteps.astype(jnp.float32)[:, None] * freq_table[None, :]
    sinus_rows = jnp.concatenate([jnp.cos(angle_rows), jnp.sin(angle_rows)], axis=1).astype(jnp.bfloat16)
    embed_one = jax.nn.silu(jnp.dot(sinus_rows, time_first, preferred_element_type=jnp.float32)).astype(jnp.bfloat16)
    embed_two = jax.nn.silu(jnp.dot(embed_one, time_second, preferred_element_type=jnp.float32)).astype(jnp.bfloat16)
    step_embed = jnp.dot(embed_two, embed_proj, preferred_element_type=jnp.float32)

    def one_step(embed_row):
        hidden = conv_out + embed_row[:, None, None, None]
        mid_act = group_silu(hidden, GROUPS).astype(jnp.bfloat16)
        second = conv_taps(jnp.pad(mid_act, ((0, 0), (0, 0), (1, 1), (0, 0))), conv_second)
        temporal_in = jax.nn.silu(second).astype(jnp.bfloat16)
        framed = jnp.pad(temporal_in, ((0, 0), (1, 1), (0, 0), (0, 0))).astype(jnp.float32)
        frame_count = second.shape[1]
        mixed_out = second
        for offset in range(3):
            mixed_out = mixed_out + jnp.einsum('oi,ifhw->ofhw', temporal_weight[offset].astype(jnp.float32), framed[:, offset:offset + frame_count])
        return (skip_out + mixed_out).astype(jnp.bfloat16)
    return lax.map(one_step, step_embed)
```

```python
import functools
import math

import jax
import jax.numpy as jnp
from jax import lax
from jax.experimental import pallas as pl
from jax.experimental.pallas import tpu as pltpu
from jax.sharding import PartitionSpec as P

GROUPS = 32


norm_eps = 1e-05


def with_halo(cells, sides, width):
    for axis, dim in sides:
        count = lax.axis_size(axis)
        ends = count - 1
        head = lax.slice_in_dim(cells, 0, width, axis=dim)
        tail = lax.slice_in_dim(cells, cells.shape[dim] - width, cells.shape[dim], axis=dim)
        cells = jnp.concatenate(
            [
                lax.ppermute(tail, axis, [(i, (i + 1) % count) for i in range(ends)]),
                cells,
                lax.ppermute(head, axis, [((i + 1) % count, i) for i in range(ends)]),
            ],
            axis=dim,
        )
    return cells


def conv_taps(padded, weights):
    row_count = padded.shape[2] - 2
    col_count = padded.shape[3]
    padded_cols = jnp.pad(padded, ((0, 0), (0, 0), (0, 0), (1, 1)))
    running = jnp.zeros((weights.shape[2], padded.shape[1], row_count, col_count), jnp.float32)
    for row_off in range(3):
        for col_off in range(3):
            window = padded_cols[:, :, row_off : row_off + row_count, col_off : col_off + col_count]
            running = running + jnp.einsum(
                "oi,ifhw->ofhw",
                weights[row_off, col_off],
                window,
                preferred_element_type=jnp.float32,
            )
    return running


def channel_scales(sum_one, sum_two, groups, count_all):
    per_group = sum_one.shape[0] // groups
    mean_group = sum_one.reshape(groups, per_group).sum(axis=1) / count_all
    square_group = sum_two.reshape(groups, per_group).sum(axis=1) / count_all
    rstd_group = lax.rsqrt(square_group - mean_group * mean_group + norm_eps)
    return (jnp.repeat(mean_group, per_group), jnp.repeat(rstd_group, per_group))


def on_device(
    enc_feats,
    skip_feats,
    timesteps,
    time_first,
    time_second,
    embed_proj,
    conv_first,
    conv_second,
    temporal_weight,
    skip_weight,
):
    channels = conv_second.shape[2]
    own_chans = enc_feats.shape[0]
    frames = enc_feats.shape[1]
    row_count = enc_feats.shape[2]
    col_count = enc_feats.shape[3]
    spread = lax.axis_size("frame") * lax.axis_size("strip")
    chan_start = lax.axis_index("step") * own_chans
    stacked = jnp.stack([enc_feats, skip_feats])
    wide_feats = stacked.astype(jnp.float32)
    local_one = jnp.sum(wide_feats, axis=(2, 3, 4))
    local_two = jnp.sum(wide_feats * wide_feats, axis=(2, 3, 4))
    anchor = jnp.zeros((), jnp.int32)
    place_one = lax.dynamic_update_slice(
        jnp.zeros((2, channels), jnp.float32), local_one, (anchor, chan_start)
    )
    place_two = lax.dynamic_update_slice(
        jnp.zeros((2, channels), jnp.float32), local_two, (anchor, chan_start)
    )
    total_one, total_two = lax.psum((place_one, place_two), ("step", "frame", "strip"))
    in_count = frames * row_count * col_count * spread * (2 * channels // GROUPS)
    mean_in, rstd_in = channel_scales(
        total_one.reshape(-1), total_two.reshape(-1), GROUPS, in_count
    )
    rimmed = with_halo(stacked, (("strip", 3),), 1)
    strip_at = lax.axis_index("strip")
    strip_last = lax.axis_size("strip") - 1
    positions = jnp.arange(row_count + 2)
    row_keep = (
        ((positions > 0) | (strip_at > 0)) & ((positions < row_count + 1) | (strip_at < strip_last))
    ).astype(jnp.float32)
    pieces = lax.all_gather(rimmed, "step", axis=1, tiled=True)
    chans_here = pieces.shape[1]
    mean_rows = jnp.stack(
        [
            lax.slice_in_dim(mean_in, 0, chans_here, axis=0),
            lax.dynamic_slice_in_dim(mean_in, channels, chans_here),
        ]
    )
    rstd_rows = jnp.stack(
        [
            lax.slice_in_dim(rstd_in, 0, chans_here, axis=0),
            lax.dynamic_slice_in_dim(rstd_in, channels, chans_here),
        ]
    )
    normed = jax.nn.silu(
        (pieces.astype(jnp.float32) - mean_rows[:, :, None, None, None])
        * rstd_rows[:, :, None, None, None]
    )
    normed = normed * row_keep[None, None, None, :, None]
    act_rows = normed.astype(jnp.bfloat16).reshape(2 * chans_here, frames, row_count + 2, col_count)
    tap_weights = jnp.concatenate(
        [
            lax.slice_in_dim(conv_first, 0, chans_here, axis=3),
            lax.dynamic_slice_in_dim(conv_first, channels, chans_here, 3),
        ],
        axis=3,
    )
    skip_cols = jnp.concatenate(
        [
            lax.slice_in_dim(skip_weight, 0, chans_here, axis=1),
            lax.dynamic_slice_in_dim(skip_weight, channels, chans_here, 1),
        ],
        axis=1,
    )
    inner_rows = pieces[:, :, :, 1 : row_count + 1].reshape(
        2 * chans_here, frames, row_count, col_count
    )
    conv_part = conv_taps(act_rows, tap_weights)
    skip_part = jnp.einsum(
        "oi,ifhw->ofhw", skip_cols, inner_rows, preferred_element_type=jnp.float32
    )
    half_chans = channels // 2
    freq_table = jnp.exp(
        -math.log(10000.0) * jnp.arange(half_chans, dtype=jnp.float32) / half_chans
    )
    angle_rows = timesteps.astype(jnp.float32)[:, None] * freq_table[None, :]
    sinus_rows = jnp.concatenate([jnp.cos(angle_rows), jnp.sin(angle_rows)], axis=1).astype(
        jnp.bfloat16
    )
    embed_one = jax.nn.silu(
        jnp.dot(sinus_rows, time_first, preferred_element_type=jnp.float32)
    ).astype(jnp.bfloat16)
    embed_two = jax.nn.silu(
        jnp.dot(embed_one, time_second, preferred_element_type=jnp.float32)
    ).astype(jnp.bfloat16)
    step_embed = jnp.dot(embed_two, embed_proj, preferred_element_type=jnp.float32)
    hidden = conv_part + step_embed[0][:, None, None, None]
    hidden_one = jnp.sum(hidden, axis=(1, 2, 3))
    hidden_two = jnp.sum(hidden * hidden, axis=(1, 2, 3))
    total_hone, total_htwo = lax.psum((hidden_one, hidden_two), ("frame", "strip"))
    mid_count = frames * row_count * col_count * spread * (channels // GROUPS)
    mean_mid, rstd_mid = channel_scales(total_hone, total_htwo, GROUPS, mid_count)
    mid_act = jax.nn.silu(
        (hidden - mean_mid[:, None, None, None]) * rstd_mid[:, None, None, None]
    ).astype(jnp.bfloat16)
    mid_rim = with_halo(mid_act, (("strip", 2),), 1)
    second = conv_taps(mid_rim, conv_second)
    temporal_in = jax.nn.silu(second).astype(jnp.bfloat16)
    framed = with_halo(temporal_in, (("frame", 1),), 1)
    mixed_out = second
    for offset in range(3):
        mixed_out = mixed_out + jnp.einsum(
            "oi,ifhw->ofhw",
            temporal_weight[offset],
            framed[:, offset : offset + frames],
            preferred_element_type=jnp.float32,
        )
    decoded = (skip_part + mixed_out).astype(jnp.bfloat16)
    return decoded[None]


MESH = pl.DeviceIdType.MESH
HIGH = lax.Precision.HIGHEST


def silu(v):
    h = 0.5 * v
    return h + h * jnp.tanh(h)


def lane_dot(a, b):
    return lax.dot_general(
        a, b, (((1,), (1,)), ((), ())), precision=HIGH, preferred_element_type=jnp.float32
    )


def one_hot(shape, dim, per_group, offset):
    chan = lax.broadcasted_iota(jnp.int32, shape, dim)
    group = lax.broadcasted_iota(jnp.int32, shape, 1 - dim) - offset
    low = group * per_group
    return jnp.where((chan >= low) & (chan < low + per_group), 1.0, 0.0).astype(jnp.float32)


def pack_sums(one, two, per_group):
    count = one.shape[0]
    groups = count // per_group
    tall = jnp.dot(
        one_hot((128, count), 1, per_group, 0), one, precision=HIGH, preferred_element_type=jnp.float32
    ) + jnp.dot(
        one_hot((128, count), 1, per_group, groups), two, precision=HIGH, preferred_element_type=jnp.float32
    )
    return lane_dot(jnp.ones((8, 128), jnp.float32), tall)


def columns_of(total, count, per_group, entries):
    groups = count // per_group
    mean = lane_dot(one_hot((count, 128), 0, per_group, 0), total)[:, :1] / entries
    square = lane_dot(one_hot((count, 128), 0, per_group, groups), total)[:, :1] / entries
    rstd = lax.rsqrt(square - mean * mean + norm_eps)
    return jnp.broadcast_to(mean, (count, 128)), jnp.broadcast_to(rstd, (count, 128))


def push(src, dst, send, recv, axis, target):
    return pltpu.make_async_remote_copy(
        src_ref=src, dst_ref=dst, send_sem=send, recv_sem=recv,
        device_id={axis: target}, device_id_type=MESH,
    )


def sum_over(axis, n, src, slots, send, recv):
    me = lax.axis_index(axis)
    copies = [
        push(src, slots.at[d - 1], send.at[d - 1], recv.at[d - 1], axis, lax.rem(me + d, n))
        for d in range(1, n)
    ]
    for copy in copies:
        copy.start()
    total = src[...]
    for d, copy in enumerate(copies):
        copy.wait_recv()
        total = total + slots[d]
    for copy in copies:
        copy.wait_send()
    return total


def put_taps(value, store):
    lane = lax.broadcasted_iota(jnp.int32, value.shape, 1)
    store(0, jnp.where(lane == 0, 0.0, pltpu.roll(value, 1, 1)).astype(jnp.bfloat16))
    store(1, value.astype(jnp.bfloat16))
    store(2, jnp.where(lane == 127, 0.0, pltpu.roll(value, 127, 1)).astype(jnp.bfloat16))


def block_kernel(
    sizes,
    feats, sinus, first_h, second_h, proj_h, conv1_h, conv2_h, temp_h, skip_h,
    out,
    raw, act, hid, act2, tbuf, acc1, acc2, cols_in, cols_mid, emb,
    w1, w2raw, w2, wtraw, wt, ws, tf, ts, ep,
    stats, slots_strip, slots_frame, slot_step,
    wsem, own_sem, x_send, x_recv, h_send, h_recv, g_send, g_recv, m_send, m_recv,
    t_send, t_recv, ss_send, ss_recv, sf_send, sf_recv, sx_send, sx_recv,
):
    n_frame, n_strip = sizes
    rows, own = feats.shape[0], feats.shape[2]
    chans = 2 * own
    last = rows - 1
    step, frame, strip = (lax.axis_index(a) for a in ("step", "frame", "strip"))
    partner = 1 - step
    mine = pl.ds(pl.multiple_of(step * own, 16), own)
    theirs = pl.ds(pl.multiple_of(partner * own, 16), own)

    loads = [
        pltpu.make_async_copy(conv1_h.at[t // 3, t % 3], w1.at[:, pl.ds(t * 2 * chans, 2 * chans)], wsem.at[t])
        for t in range(9)
    ]
    small = [
        pltpu.make_async_copy(src, dst, wsem.at[9 + i])
        for i, (src, dst) in enumerate(
            ((first_h, tf), (second_h, ts), (proj_h, ep), (conv2_h, w2raw), (temp_h, wtraw), (skip_h, ws))
        )
    ]
    keep = pltpu.make_async_copy(feats, raw.at[pl.ds(1, rows), :, mine, :], own_sem)
    keep.start()

    barrier = pltpu.get_barrier_semaphore()
    for axis, n in (("step", 2), ("frame", n_frame), ("strip", n_strip)):
        for d in range(1, n):
            pl.semaphore_signal(
                barrier, inc=1, device_id={axis: lax.rem(lax.axis_index(axis) + d, n)}, device_id_type=MESH
            )
    pl.semaphore_wait(barrier, 1 + n_frame - 1 + n_strip - 1)

    def row_copy(r):
        return push(feats.at[r], raw.at[r + 1, :, mine, :], x_send.at[r], x_recv.at[r], "step", partner)

    def own_up():
        return push(feats.at[0], raw.at[rows + 1, :, mine, :], h_send.at[1], h_recv.at[1], "strip", strip - 1)

    def own_down():
        return push(feats.at[last], raw.at[0, :, mine, :], h_send.at[0], h_recv.at[0], "strip", strip + 1)

    def far_up():
        return push(
            raw.at[1, :, theirs, :], raw.at[rows + 1, :, theirs, :], g_send.at[1], g_recv.at[1], "strip", strip - 1
        )

    def far_down():
        return push(
            raw.at[rows, :, theirs, :], raw.at[0, :, theirs, :], g_send.at[0], g_recv.at[0], "strip", strip + 1
        )

    has_up, has_down = strip > 0, strip < n_strip - 1
    for r in (0, last):
        row_copy(r).start()
    pl.when(has_up)(lambda: own_up().start())
    pl.when(has_down)(lambda: own_down().start())

    @pl.loop(1, last)
    def _(r):
        row_copy(r).start()

    for load in loads + small:
        load.start()

    acc1[...] = jnp.zeros_like(acc1)
    acc2[...] = jnp.zeros_like(acc2)

    @pl.loop(0, rows)
    def _(r):
        for h in range(2):
            wide = feats[r, h].astype(jnp.float32)
            a, b = wide[:, :128], wide[:, 128:]
            at = pl.ds(h * own, own)
            acc1[at, :] = acc1[at, :] + (a + b)
            acc2[at, :] = acc2[at, :] + (a * a + b * b)

    per_in = 2 * chans // GROUPS
    stats[0] = pack_sums(acc1[...], acc2[...], per_in)
    stats[1] = sum_over("strip", n_strip, stats.at[0], slots_strip.at[0], ss_send.at[0], ss_recv.at[0])
    stats[2] = sum_over("frame", n_frame, stats.at[1], slots_frame.at[0], sf_send.at[0], sf_recv.at[0])
    swap = push(stats.at[2], slot_step, sx_send, sx_recv, "step", partner)
    swap.start()
    entries = 2 * rows * 128 * n_frame * n_strip
    in_entries = float(entries * per_in)

    def set_cols(total, at):
        mean, rstd = columns_of(total, chans, per_in, in_entries)
        for h in range(2):
            cols_in[0, h, at, :] = mean[h * own : (h + 1) * own]
            cols_in[1, h, at, :] = rstd[h * own : (h + 1) * own]

    set_cols(stats[2], mine)

    def make_act(r, at):
        for h in range(2):
            mean, rstd = cols_in[0, h, at, :], cols_in[1, h, at, :]
            for f in range(2):
                lanes = pl.ds(f * 128, 128)
                value = silu((raw[r, h, at, lanes].astype(jnp.float32) - mean) * rstd)

                def store(t, v):
                    act[r, t, h, at, lanes] = v

                put_taps(value, store)

    keep.wait()

    @pl.loop(1, rows + 1)
    def _(r):
        make_act(r, mine)

    @pl.when(has_up)
    def _():
        own_down().wait_recv()
        make_act(0, mine)

    @pl.when(has_down)
    def _():
        own_up().wait_recv()
        make_act(rows + 1, mine)

    @pl.when(strip == 0)
    def _():
        act[0] = jnp.zeros(act.shape[1:], jnp.bfloat16)

    @pl.when(strip == n_strip - 1)
    def _():
        act[rows + 1] = jnp.zeros(act.shape[1:], jnp.bfloat16)

    swap.wait()
    set_cols(slot_step[...], theirs)

    for load in small:
        load.wait()
    one = silu(jnp.dot(sinus[...], tf[...], preferred_element_type=jnp.float32)).astype(jnp.bfloat16)
    two = silu(jnp.dot(one, ts[...], preferred_element_type=jnp.float32)).astype(jnp.bfloat16)
    embed = jnp.dot(two, ep[...], preferred_element_type=jnp.float32)
    emb[...] = jnp.broadcast_to(
        lane_dot(one_hot((chans, chans), 0, 1, 0), embed[:8])[:, :1], (chans, 128)
    )
    for t in range(9):
        w2[:, t * chans : (t + 1) * chans] = w2raw[t // 3, t % 3]
    for t in range(3):
        wt[:, t * chans : (t + 1) * chans] = wtraw[t]
    for load in loads:
        load.wait()

    def arrive(r):
        row_copy(r).wait_recv()
        make_act(r + 1, theirs)

    arrive(0)
    pl.when(has_up)(lambda: far_up().start())
    arrive(last)
    pl.when(has_down)(lambda: far_down().start())
    arrive(1)
    acc1[...] = jnp.zeros_like(acc1)
    acc2[...] = jnp.zeros_like(acc2)

    @pl.loop(0, rows)
    def _(i):
        high = i // 4
        three = (i // 3) % 2 * (1 - high)
        c = (i + 1) * (1 - high) * (1 - three) + i * high

        @pl.when((i < 3) | ((i > 3) & (i < rows - 2)))
        def _():
            arrive(c + 1)

        @pl.when((i == 3) & has_up)
        def _():
            far_down().wait_recv()
            make_act(0, theirs)

        @pl.when((i == 3) & has_down)
        def _():
            far_up().wait_recv()
            make_act(rows + 1, theirs)

        window = act[pl.ds(c, 3)].reshape(18 * chans, 256)
        found = jnp.dot(w1[...], window, preferred_element_type=jnp.float32)
        a, b = found[:, :128] + emb[...], found[:, 128:] + emb[...]
        hid[c, :, :128] = a
        hid[c, :, 128:] = b
        acc1[...] = acc1[...] + (a + b)
        acc2[...] = acc2[...] + (a * a + b * b)

    per_mid = chans // GROUPS
    stats[3] = pack_sums(acc1[...], acc2[...], per_mid)
    stats[4] = sum_over("strip", n_strip, stats.at[3], slots_strip.at[1], ss_send.at[1], ss_recv.at[1])
    total = sum_over("frame", n_frame, stats.at[4], slots_frame.at[1], sf_send.at[1], sf_recv.at[1])
    mean, rstd = columns_of(total, chans, per_mid, float(entries * per_mid))
    cols_mid[0] = mean
    cols_mid[1] = rstd

    def mid_row(r):
        for f in range(2):
            lanes = pl.ds(f * 128, 128)
            value = silu((hid[r, :, lanes] - cols_mid[0]) * cols_mid[1])

            def store(t, v):
                act2[r + 1, t, :, lanes] = v

            put_taps(value, store)

    def mid_up():
        return push(act2.at[1, 1], act2.at[rows + 1, 1], m_send.at[1], m_recv.at[1], "strip", strip - 1)

    def mid_down():
        return push(act2.at[rows, 1], act2.at[0, 1], m_send.at[0], m_recv.at[0], "strip", strip + 1)

    mid_row(0)
    pl.when(has_up)(lambda: mid_up().start())
    mid_row(last)
    pl.when(has_down)(lambda: mid_down().start())

    @pl.loop(1, last)
    def _(r):
        mid_row(r)

    def edge_row(r):
        for f in range(2):
            lanes = pl.ds(f * 128, 128)
            value = act2[r, 1, :, lanes].astype(jnp.float32)

            def store(t, v):
                if t != 1:
                    act2[r, t, :, lanes] = v

            put_taps(value, store)

    has_prev, has_next = frame > 0, frame < n_frame - 1

    def to_prev(c):
        return push(
            tbuf.at[c, 1, :, pl.ds(0, 128)], tbuf.at[c, 2, :, pl.ds(128, 128)],
            t_send.at[0, c], t_recv.at[0, c], "frame", frame - 1,
        )

    def to_next(c):
        return push(
            tbuf.at[c, 1, :, pl.ds(128, 128)], tbuf.at[c, 0, :, pl.ds(0, 128)],
            t_send.at[1, c], t_recv.at[1, c], "frame", frame + 1,
        )

    def inner_first(i):
        tail = i // (rows - 2)
        return (i + 1) * (1 - tail) + (i - (rows - 2)) * last * tail

    @pl.loop(0, rows)
    def _(i):
        c = inner_first(i)

        @pl.when((i == rows - 2) & has_up)
        def _():
            mid_down().wait_recv()
            edge_row(0)

        @pl.when((i == rows - 2) & has_down)
        def _():
            mid_up().wait_recv()
            edge_row(rows + 1)

        @pl.when((i == rows - 2) & (strip == 0))
        def _():
            act2[0] = jnp.zeros(act2.shape[1:], jnp.bfloat16)

        @pl.when((i == rows - 2) & (strip == n_strip - 1))
        def _():
            act2[rows + 1] = jnp.zeros(act2.shape[1:], jnp.bfloat16)

        window = act2[pl.ds(c, 3)].reshape(9 * chans, 256)
        found = jnp.dot(w2[...], window, preferred_element_type=jnp.float32)
        hid[c] = found
        inner = silu(found).astype(jnp.bfloat16)
        tbuf[c, 1] = inner
        tbuf[c, 0, :, 128:] = inner[:, :128]
        tbuf[c, 2, :, :128] = inner[:, 128:]

        @pl.when(has_prev)
        def _():
            to_prev(c).start()

        @pl.when(has_next)
        def _():
            to_next(c).start()

        @pl.when(frame == 0)
        def _():
            tbuf[c, 0, :, :128] = jnp.zeros((chans, 128), jnp.bfloat16)

        @pl.when(frame == n_frame - 1)
        def _():
            tbuf[c, 2, :, 128:] = jnp.zeros((chans, 128), jnp.bfloat16)

    @pl.loop(0, rows)
    def _(i):
        c = inner_first(i)
        base = hid[c] + jnp.dot(
            ws[...], raw[c + 1].reshape(2 * chans, 256), preferred_element_type=jnp.float32
        )

        @pl.when(has_prev)
        def _():
            to_next(c).wait_recv()

        @pl.when(has_next)
        def _():
            to_prev(c).wait_recv()

        mixed = jnp.dot(
            wt[...], tbuf[c].reshape(3 * chans, 256), preferred_element_type=jnp.float32
        )
        out[c] = (base + mixed).astype(jnp.bfloat16)

    @pl.loop(0, rows)
    def _(r):
        row_copy(r).wait_send()

        @pl.when(has_prev)
        def _():
            to_prev(r).wait_send()

        @pl.when(has_next)
        def _():
            to_next(r).wait_send()

    @pl.when(has_up)
    def _():
        own_up().wait_send()
        far_up().wait_send()
        mid_up().wait_send()

    @pl.when(has_down)
    def _():
        own_down().wait_send()
        far_down().wait_send()
        mid_down().wait_send()


def in_kernel(
    enc_feats, skip_feats, timesteps, time_first, time_second, embed_proj,
    conv_first, conv_second, temporal_weight, skip_weight,
):
    own, frames, rows, cols = enc_feats.shape
    chans = conv_second.shape[2]
    width = frames * cols
    temb = time_first.shape[1]
    n_frame, n_strip = lax.axis_size("frame"), lax.axis_size("strip")
    feats = jnp.stack([enc_feats, skip_feats]).transpose(3, 0, 1, 2, 4).reshape(rows, 2, own, width)
    half_chans = chans // 2
    freq_table = jnp.exp(
        -math.log(10000.0) * jnp.arange(half_chans, dtype=jnp.float32) / half_chans
    )
    angle_rows = timesteps.astype(jnp.float32)[:, None] * freq_table[None, :]
    sinus = jnp.concatenate([jnp.cos(angle_rows), jnp.sin(angle_rows)], axis=1).astype(jnp.bfloat16)
    sinus = jnp.broadcast_to(sinus, (16, chans))
    bf16, f32 = jnp.bfloat16, jnp.float32
    dma = pltpu.SemaphoreType.DMA
    anywhere = pl.BlockSpec(memory_space=pl.ANY)
    inside = pl.BlockSpec(memory_space=pltpu.VMEM)
    pixels = rows * width
    result = pl.pallas_call(
        functools.partial(block_kernel, (n_frame, n_strip)),
        out_shape=jax.ShapeDtypeStruct((rows, chans, width), bf16),
        in_specs=[inside, inside] + [anywhere] * 7,
        out_specs=inside,
        scratch_shapes=[
            pltpu.VMEM((rows + 2, 2, chans, width), bf16),
            pltpu.VMEM((rows + 2, 3, 2, chans, width), bf16),
            pltpu.VMEM((rows, chans, width), f32),
            pltpu.VMEM((rows + 2, 3, chans, width), bf16),
            pltpu.VMEM((rows, 3, chans, width), bf16),
            pltpu.VMEM((chans, 128), f32),
            pltpu.VMEM((chans, 128), f32),
            pltpu.VMEM((2, 2, chans, 128), f32),
            pltpu.VMEM((2, chans, 128), f32),
            pltpu.VMEM((chans, 128), f32),
            pltpu.VMEM((chans, 18 * chans), bf16),
            pltpu.VMEM((3, 3, chans, chans), bf16),
            pltpu.VMEM((chans, 9 * chans), bf16),
            pltpu.VMEM((3, chans, chans), bf16),
            pltpu.VMEM((chans, 3 * chans), bf16),
            pltpu.VMEM((chans, 2 * chans), bf16),
            pltpu.VMEM((chans, temb), bf16),
            pltpu.VMEM((temb, temb), bf16),
            pltpu.VMEM((temb, chans), bf16),
            pltpu.VMEM((5, 8, 128), f32),
            pltpu.VMEM((2, n_strip - 1, 8, 128), f32),
            pltpu.VMEM((2, n_frame - 1, 8, 128), f32),
            pltpu.VMEM((8, 128), f32),
            dma((15,)), dma,
            dma((rows,)), dma((rows,)),
            dma((2,)), dma((2,)), dma((2,)), dma((2,)), dma((2,)), dma((2,)),
            dma((2, rows)), dma((2, rows)),
            dma((2, n_strip - 1)), dma((2, n_strip - 1)),
            dma((2, n_frame - 1)), dma((2, n_frame - 1)),
            dma, dma,
        ],
        compiler_params=pltpu.CompilerParams(
            collective_id=0, has_side_effects=True, vmem_limit_bytes=58 * 2**20
        ),
        cost_estimate=pl.CostEstimate(
            flops=2 * pixels * chans * chans * (18 + 9 + 3 + 2),
            bytes_accessed=14 * 2**20,
            transcendentals=pixels * chans * 4,
        ),
    )(feats, sinus, time_first, time_second, embed_proj, conv_first, conv_second, temporal_weight, skip_weight)
    return result.reshape(rows, chans, frames, cols).transpose(1, 2, 0, 3)[None]


def block(*args):
    own, frames, rows, cols = args[0].shape
    fits = (
        lax.axis_size("step") == 2
        and own % 16 == 0
        and args[7].shape[2] == 2 * own
        and (own * 4) % GROUPS == 0
        and own % (own * 4 // GROUPS) == 0
        and frames == 2
        and rows == 8
        and cols == 128
    )
    return in_kernel(*args) if fits else on_device(*args)


def solution(mesh):
    return jax.shard_map(
        block,
        mesh=mesh,
        in_specs=(
            P("step", "frame", "strip", None),
            P("step", "frame", "strip", None),
            P("step"),
            P(),
            P(),
            P(),
            P(),
            P(),
            P(),
            P(),
        ),
        out_specs=P("step", None, "frame", "strip", None),
        check_vma=False,
    )
```

```python
import functools
import math

import jax
import jax.numpy as jnp
from jax import lax
from jax.experimental import pallas as pl
from jax.experimental.pallas import tpu as pltpu
from jax.sharding import PartitionSpec as P

GROUPS = 32


norm_eps = 1e-05


def with_halo(cells, sides, width):
    for axis, dim in sides:
        count = lax.axis_size(axis)
        ends = count - 1
        head = lax.slice_in_dim(cells, 0, width, axis=dim)
        tail = lax.slice_in_dim(cells, cells.shape[dim] - width, cells.shape[dim], axis=dim)
        cells = jnp.concatenate(
            [
                lax.ppermute(tail, axis, [(i, (i + 1) % count) for i in range(ends)]),
                cells,
                lax.ppermute(head, axis, [((i + 1) % count, i) for i in range(ends)]),
            ],
            axis=dim,
        )
    return cells


def conv_taps(padded, weights):
    row_count = padded.shape[2] - 2
    col_count = padded.shape[3]
    padded_cols = jnp.pad(padded, ((0, 0), (0, 0), (0, 0), (1, 1)))
    running = jnp.zeros((weights.shape[2], padded.shape[1], row_count, col_count), jnp.float32)
    for row_off in range(3):
        for col_off in range(3):
            window = padded_cols[:, :, row_off : row_off + row_count, col_off : col_off + col_count]
            running = running + jnp.einsum(
                "oi,ifhw->ofhw",
                weights[row_off, col_off],
                window,
                preferred_element_type=jnp.float32,
            )
    return running


def channel_scales(sum_one, sum_two, groups, count_all):
    per_group = sum_one.shape[0] // groups
    mean_group = sum_one.reshape(groups, per_group).sum(axis=1) / count_all
    square_group = sum_two.reshape(groups, per_group).sum(axis=1) / count_all
    rstd_group = lax.rsqrt(square_group - mean_group * mean_group + norm_eps)
    return (jnp.repeat(mean_group, per_group), jnp.repeat(rstd_group, per_group))


def on_device(
    enc_feats,
    skip_feats,
    timesteps,
    time_first,
    time_second,
    embed_proj,
    conv_first,
    conv_second,
    temporal_weight,
    skip_weight,
):
    channels = conv_second.shape[2]
    own_chans = enc_feats.shape[0]
    frames = enc_feats.shape[1]
    row_count = enc_feats.shape[2]
    col_count = enc_feats.shape[3]
    spread = lax.axis_size("frame") * lax.axis_size("strip")
    chan_start = lax.axis_index("step") * own_chans
    stacked = jnp.stack([enc_feats, skip_feats])
    wide_feats = stacked.astype(jnp.float32)
    local_one = jnp.sum(wide_feats, axis=(2, 3, 4))
    local_two = jnp.sum(wide_feats * wide_feats, axis=(2, 3, 4))
    anchor = jnp.zeros((), jnp.int32)
    place_one = lax.dynamic_update_slice(
        jnp.zeros((2, channels), jnp.float32), local_one, (anchor, chan_start)
    )
    place_two = lax.dynamic_update_slice(
        jnp.zeros((2, channels), jnp.float32), local_two, (anchor, chan_start)
    )
    total_one, total_two = lax.psum((place_one, place_two), ("step", "frame", "strip"))
    in_count = frames * row_count * col_count * spread * (2 * channels // GROUPS)
    mean_in, rstd_in = channel_scales(
        total_one.reshape(-1), total_two.reshape(-1), GROUPS, in_count
    )
    rimmed = with_halo(stacked, (("strip", 3),), 1)
    strip_at = lax.axis_index("strip")
    strip_last = lax.axis_size("strip") - 1
    positions = jnp.arange(row_count + 2)
    row_keep = (
        ((positions > 0) | (strip_at > 0)) & ((positions < row_count + 1) | (strip_at < strip_last))
    ).astype(jnp.float32)
    pieces = lax.all_gather(rimmed, "step", axis=1, tiled=True)
    chans_here = pieces.shape[1]
    mean_rows = jnp.stack(
        [
            lax.slice_in_dim(mean_in, 0, chans_here, axis=0),
            lax.dynamic_slice_in_dim(mean_in, channels, chans_here),
        ]
    )
    rstd_rows = jnp.stack(
        [
            lax.slice_in_dim(rstd_in, 0, chans_here, axis=0),
            lax.dynamic_slice_in_dim(rstd_in, channels, chans_here),
        ]
    )
    normed = jax.nn.silu(
        (pieces.astype(jnp.float32) - mean_rows[:, :, None, None, None])
        * rstd_rows[:, :, None, None, None]
    )
    normed = normed * row_keep[None, None, None, :, None]
    act_rows = normed.astype(jnp.bfloat16).reshape(2 * chans_here, frames, row_count + 2, col_count)
    tap_weights = jnp.concatenate(
        [
            lax.slice_in_dim(conv_first, 0, chans_here, axis=3),
            lax.dynamic_slice_in_dim(conv_first, channels, chans_here, 3),
        ],
        axis=3,
    )
    skip_cols = jnp.concatenate(
        [
            lax.slice_in_dim(skip_weight, 0, chans_here, axis=1),
            lax.dynamic_slice_in_dim(skip_weight, channels, chans_here, 1),
        ],
        axis=1,
    )
    inner_rows = pieces[:, :, :, 1 : row_count + 1].reshape(
        2 * chans_here, frames, row_count, col_count
    )
    conv_part = conv_taps(act_rows, tap_weights)
    skip_part = jnp.einsum(
        "oi,ifhw->ofhw", skip_cols, inner_rows, preferred_element_type=jnp.float32
    )
    half_chans = channels // 2
    freq_table = jnp.exp(
        -math.log(10000.0) * jnp.arange(half_chans, dtype=jnp.float32) / half_chans
    )
    angle_rows = timesteps.astype(jnp.float32)[:, None] * freq_table[None, :]
    sinus_rows = jnp.concatenate([jnp.cos(angle_rows), jnp.sin(angle_rows)], axis=1).astype(
        jnp.bfloat16
    )
    embed_one = jax.nn.silu(
        jnp.dot(sinus_rows, time_first, preferred_element_type=jnp.float32)
    ).astype(jnp.bfloat16)
    embed_two = jax.nn.silu(
        jnp.dot(embed_one, time_second, preferred_element_type=jnp.float32)
    ).astype(jnp.bfloat16)
    step_embed = jnp.dot(embed_two, embed_proj, preferred_element_type=jnp.float32)
    hidden = conv_part + step_embed[0][:, None, None, None]
    hidden_one = jnp.sum(hidden, axis=(1, 2, 3))
    hidden_two = jnp.sum(hidden * hidden, axis=(1, 2, 3))
    total_hone, total_htwo = lax.psum((hidden_one, hidden_two), ("frame", "strip"))
    mid_count = frames * row_count * col_count * spread * (channels // GROUPS)
    mean_mid, rstd_mid = channel_scales(total_hone, total_htwo, GROUPS, mid_count)
    mid_act = jax.nn.silu(
        (hidden - mean_mid[:, None, None, None]) * rstd_mid[:, None, None, None]
    ).astype(jnp.bfloat16)
    mid_rim = with_halo(mid_act, (("strip", 2),), 1)
    second = conv_taps(mid_rim, conv_second)
    temporal_in = jax.nn.silu(second).astype(jnp.bfloat16)
    framed = with_halo(temporal_in, (("frame", 1),), 1)
    mixed_out = second
    for offset in range(3):
        mixed_out = mixed_out + jnp.einsum(
            "oi,ifhw->ofhw",
            temporal_weight[offset],
            framed[:, offset : offset + frames],
            preferred_element_type=jnp.float32,
        )
    decoded = (skip_part + mixed_out).astype(jnp.bfloat16)
    return decoded[None]


MESH = pl.DeviceIdType.MESH
HIGH = lax.Precision.HIGHEST


def silu(v):
    h = 0.5 * v
    return h + h * jnp.tanh(h)


def lane_dot(a, b):
    return lax.dot_general(
        a, b, (((1,), (1,)), ((), ())), precision=HIGH, preferred_element_type=jnp.float32
    )


def one_hot(shape, dim, per_group, offset):
    chan = lax.broadcasted_iota(jnp.int32, shape, dim)
    group = lax.broadcasted_iota(jnp.int32, shape, 1 - dim) - offset
    low = group * per_group
    return jnp.where((chan >= low) & (chan < low + per_group), 1.0, 0.0).astype(jnp.float32)


def pack_sums(one, two, per_group):
    count = one.shape[0]
    groups = count // per_group
    tall = jnp.dot(
        one_hot((128, count), 1, per_group, 0), one, precision=HIGH, preferred_element_type=jnp.float32
    ) + jnp.dot(
        one_hot((128, count), 1, per_group, groups), two, precision=HIGH, preferred_element_type=jnp.float32
    )
    return lane_dot(jnp.ones((8, 128), jnp.float32), tall)


def columns_of(total, count, per_group, entries):
    groups = count // per_group
    mean = lane_dot(one_hot((count, 128), 0, per_group, 0), total)[:, :1] / entries
    square = lane_dot(one_hot((count, 128), 0, per_group, groups), total)[:, :1] / entries
    rstd = lax.rsqrt(square - mean * mean + norm_eps)
    return jnp.broadcast_to(mean, (count, 128)), jnp.broadcast_to(rstd, (count, 128))


def push(src, dst, send, recv, axis, target):
    return pltpu.make_async_remote_copy(
        src_ref=src, dst_ref=dst, send_sem=send, recv_sem=recv,
        device_id={axis: target}, device_id_type=MESH,
    )


def sum_over(axis, n, src, slots, send, recv):
    me = lax.axis_index(axis)
    copies = [
        push(src, slots.at[d - 1], send.at[d - 1], recv.at[d - 1], axis, lax.rem(me + d, n))
        for d in range(1, n)
    ]
    for copy in copies:
        copy.start()
    total = src[...]
    for d, copy in enumerate(copies):
        copy.wait_recv()
        total = total + slots[d]
    for copy in copies:
        copy.wait_send()
    return total


def join_taps(found, chans, f):
    lanes = slice(f * 128, f * 128 + 128)
    lane = lax.broadcasted_iota(jnp.int32, (chans, 128), 1)
    before = pltpu.roll(found[:chans, lanes], 1, 1)
    after = pltpu.roll(found[2 * chans :, lanes], 127, 1)
    return (
        found[chans : 2 * chans, lanes]
        + jnp.where(lane == 0, 0.0, before)
        + jnp.where(lane == 127, 0.0, after)
    )


def block_kernel(
    sizes,
    enc, skip, sinus, first_h, second_h, proj_h, conv1_h, conv2_h, temp_h, skip_h,
    out,
    raw, act, hid, act2, tbuf, acc1, acc2, cols_in, cols_mid, emb,
    w1, w2raw, w2, wtraw, wt, ws, tf, ts, ep,
    stats, slots_strip, slots_frame, slot_step,
    wsem, own_sem, x_send, x_recv, h_send, h_recv, g_send, g_recv, m_send, m_recv,
    t_send, t_recv, ss_send, ss_recv, sf_send, sf_recv, sx_send, sx_recv,
):
    n_frame, n_strip = sizes
    rows, own = enc.shape[1], enc.shape[2]
    chans = 2 * own
    last = rows - 1
    step, frame, strip = (lax.axis_index(a) for a in ("step", "frame", "strip"))
    partner = 1 - step
    mine = pl.ds(pl.multiple_of(step * own, 16), own)
    theirs = pl.ds(pl.multiple_of(partner * own, 16), own)

    loads = [
        pltpu.make_async_copy(conv1_h.at[t // 3, t % 3], w1.at[pl.ds(t % 3 * chans, chans), pl.ds(t // 3 * 2 * chans, 2 * chans)], wsem.at[t])
        for t in range(9)
    ]
    small = [
        pltpu.make_async_copy(src, dst, wsem.at[9 + i])
        for i, (src, dst) in enumerate(
            ((first_h, tf), (second_h, ts), (proj_h, ep), (conv2_h, w2raw), (temp_h, wtraw), (skip_h, ws))
        )
    ]
    keeps = [
        pltpu.make_async_copy(
            source.at[f], raw.at[pl.ds(1, rows), h, mine, pl.ds(f * 128, 128)], own_sem.at[h, f]
        )
        for h, source in enumerate((enc, skip))
        for f in range(2)
    ]
    for keep in keeps:
        keep.start()

    barrier = pltpu.get_barrier_semaphore()
    for axis, n in (("step", 2), ("frame", n_frame), ("strip", n_strip)):
        for d in range(1, n):
            pl.semaphore_signal(
                barrier, inc=1, device_id={axis: lax.rem(lax.axis_index(axis) + d, n)}, device_id_type=MESH
            )
    pl.semaphore_wait(barrier, 1 + n_frame - 1 + n_strip - 1)
    for keep in keeps:
        keep.wait()

    def row_copy(r):
        return push(raw.at[r + 1, :, mine, :], raw.at[r + 1, :, mine, :], x_send.at[r], x_recv.at[r], "step", partner)

    def own_up():
        return push(raw.at[1, :, mine, :], raw.at[rows + 1, :, mine, :], h_send.at[1], h_recv.at[1], "strip", strip - 1)

    def own_down():
        return push(raw.at[rows, :, mine, :], raw.at[0, :, mine, :], h_send.at[0], h_recv.at[0], "strip", strip + 1)

    def far_up():
        return push(
            raw.at[1, :, theirs, :], raw.at[rows + 1, :, theirs, :], g_send.at[1], g_recv.at[1], "strip", strip - 1
        )

    def far_down():
        return push(
            raw.at[rows, :, theirs, :], raw.at[0, :, theirs, :], g_send.at[0], g_recv.at[0], "strip", strip + 1
        )

    has_up, has_down = strip > 0, strip < n_strip - 1
    for r in (0, last):
        row_copy(r).start()
    pl.when(has_up)(lambda: own_up().start())
    pl.when(has_down)(lambda: own_down().start())

    @pl.loop(1, last)
    def _(r):
        row_copy(r).start()

    for load in loads + small:
        load.start()

    acc1[...] = jnp.zeros_like(acc1)
    acc2[...] = jnp.zeros_like(acc2)

    @pl.loop(0, rows)
    def _(r):
        for h in range(2):
            wide = raw[r + 1, h, mine, :].astype(jnp.float32)
            a, b = wide[:, :128], wide[:, 128:]
            at = pl.ds(h * own, own)
            acc1[at, :] = acc1[at, :] + (a + b)
            acc2[at, :] = acc2[at, :] + (a * a + b * b)

    per_in = 2 * chans // GROUPS
    stats[0] = pack_sums(acc1[...], acc2[...], per_in)
    stats[1] = sum_over("strip", n_strip, stats.at[0], slots_strip.at[0], ss_send.at[0], ss_recv.at[0])
    stats[2] = sum_over("frame", n_frame, stats.at[1], slots_frame.at[0], sf_send.at[0], sf_recv.at[0])
    swap = push(stats.at[2], slot_step, sx_send, sx_recv, "step", partner)
    swap.start()
    entries = 2 * rows * 128 * n_frame * n_strip
    in_entries = float(entries * per_in)

    def set_cols(total, at):
        mean, rstd = columns_of(total, chans, per_in, in_entries)
        for h in range(2):
            cols_in[0, h, at, :] = mean[h * own : (h + 1) * own]
            cols_in[1, h, at, :] = rstd[h * own : (h + 1) * own]

    set_cols(stats[2], mine)

    def make_act(r, at):
        for h in range(2):
            mean, rstd = cols_in[0, h, at, :], cols_in[1, h, at, :]
            for f in range(2):
                lanes = pl.ds(f * 128, 128)
                value = silu((raw[r, h, at, lanes].astype(jnp.float32) - mean) * rstd)
                act[r, h, at, lanes] = value.astype(jnp.bfloat16)

    @pl.loop(1, rows + 1)
    def _(r):
        make_act(r, mine)

    @pl.when(has_up)
    def _():
        own_down().wait_recv()
        make_act(0, mine)

    @pl.when(has_down)
    def _():
        own_up().wait_recv()
        make_act(rows + 1, mine)

    @pl.when(strip == 0)
    def _():
        act[0] = jnp.zeros(act.shape[1:], jnp.bfloat16)

    @pl.when(strip == n_strip - 1)
    def _():
        act[rows + 1] = jnp.zeros(act.shape[1:], jnp.bfloat16)

    swap.wait()
    set_cols(slot_step[...], theirs)

    for load in small:
        load.wait()
    one = silu(jnp.dot(sinus[...], tf[...], preferred_element_type=jnp.float32)).astype(jnp.bfloat16)
    two = silu(jnp.dot(one, ts[...], preferred_element_type=jnp.float32)).astype(jnp.bfloat16)
    embed = lax.dot_general(
        ep[...], two, (((1,), (1,)), ((), ())), preferred_element_type=jnp.float32
    )
    emb[...] = jnp.broadcast_to(embed[:, :1], (chans, 128))
    for t in range(9):
        dy, dx = t // 3, t % 3
        w2[dx * chans : (dx + 1) * chans, dy * chans : (dy + 1) * chans] = w2raw[dy, dx]
    for t in range(3):
        wt[:, t * chans : (t + 1) * chans] = wtraw[t]
    for load in loads:
        load.wait()

    def arrive(r):
        row_copy(r).wait_recv()
        make_act(r + 1, theirs)

    arrive(0)
    pl.when(has_up)(lambda: far_up().start())
    arrive(last)
    pl.when(has_down)(lambda: far_down().start())
    arrive(1)
    acc1[...] = jnp.zeros_like(acc1)
    acc2[...] = jnp.zeros_like(acc2)

    @pl.loop(0, rows)
    def _(i):
        high = i // 4
        three = (i // 3) % 2 * (1 - high)
        c = (i + 1) * (1 - high) * (1 - three) + i * high

        @pl.when((i < 3) | ((i > 3) & (i < rows - 2)))
        def _():
            arrive(c + 1)

        @pl.when((i == 3) & has_up)
        def _():
            far_down().wait_recv()
            make_act(0, theirs)

        @pl.when((i == 3) & has_down)
        def _():
            far_up().wait_recv()
            make_act(rows + 1, theirs)

        window = act[pl.ds(c, 3)].reshape(6 * chans, 256)
        found = jnp.dot(w1[...], window, preferred_element_type=jnp.float32)
        a, b = join_taps(found, chans, 0) + emb[...], join_taps(found, chans, 1) + emb[...]
        hid[c, :, :128] = a
        hid[c, :, 128:] = b
        acc1[...] = acc1[...] + (a + b)
        acc2[...] = acc2[...] + (a * a + b * b)

    per_mid = chans // GROUPS
    stats[3] = pack_sums(acc1[...], acc2[...], per_mid)
    stats[4] = sum_over("strip", n_strip, stats.at[3], slots_strip.at[1], ss_send.at[1], ss_recv.at[1])
    total = sum_over("frame", n_frame, stats.at[4], slots_frame.at[1], sf_send.at[1], sf_recv.at[1])
    mean, rstd = columns_of(total, chans, per_mid, float(entries * per_mid))
    cols_mid[0] = mean
    cols_mid[1] = rstd

    def mid_row(r):
        for f in range(2):
            lanes = pl.ds(f * 128, 128)
            value = silu((hid[r, :, lanes] - cols_mid[0]) * cols_mid[1])
            act2[r + 1, :, lanes] = value.astype(jnp.bfloat16)

    def mid_up():
        return push(act2.at[1], act2.at[rows + 1], m_send.at[1], m_recv.at[1], "strip", strip - 1)

    def mid_down():
        return push(act2.at[rows], act2.at[0], m_send.at[0], m_recv.at[0], "strip", strip + 1)

    mid_row(0)
    pl.when(has_up)(lambda: mid_up().start())
    mid_row(last)
    pl.when(has_down)(lambda: mid_down().start())

    @pl.loop(1, last)
    def _(r):
        mid_row(r)

    has_prev, has_next = frame > 0, frame < n_frame - 1

    def to_prev(c):
        return push(
            tbuf.at[c, 1, :, pl.ds(0, 128)], tbuf.at[c, 2, :, pl.ds(128, 128)],
            t_send.at[0, c], t_recv.at[0, c], "frame", frame - 1,
        )

    def to_next(c):
        return push(
            tbuf.at[c, 1, :, pl.ds(128, 128)], tbuf.at[c, 0, :, pl.ds(0, 128)],
            t_send.at[1, c], t_recv.at[1, c], "frame", frame + 1,
        )

    def inner_first(i):
        tail = i // (rows - 2)
        return (i + 1) * (1 - tail) + (i - (rows - 2)) * last * tail

    @pl.loop(0, rows)
    def _(i):
        c = inner_first(i)

        @pl.when((i == rows - 2) & has_up)
        def _():
            mid_down().wait_recv()

        @pl.when((i == rows - 2) & has_down)
        def _():
            mid_up().wait_recv()

        @pl.when((i == rows - 2) & (strip == 0))
        def _():
            act2[0] = jnp.zeros(act2.shape[1:], jnp.bfloat16)

        @pl.when((i == rows - 2) & (strip == n_strip - 1))
        def _():
            act2[rows + 1] = jnp.zeros(act2.shape[1:], jnp.bfloat16)

        window = act2[pl.ds(c, 3)].reshape(3 * chans, 256)
        found = jnp.dot(w2[...], window, preferred_element_type=jnp.float32)
        for f in range(2):
            lanes = pl.ds(f * 128, 128)
            second = join_taps(found, chans, f)
            hid[c, :, lanes] = second
            inner = silu(second).astype(jnp.bfloat16)
            tbuf[c, 1, :, lanes] = inner
            tbuf[c, 2 * f, :, pl.ds(128 - f * 128, 128)] = inner

        @pl.when(has_prev)
        def _():
            to_prev(c).start()

        @pl.when(has_next)
        def _():
            to_next(c).start()

        @pl.when(frame == 0)
        def _():
            tbuf[c, 0, :, :128] = jnp.zeros((chans, 128), jnp.bfloat16)

        @pl.when(frame == n_frame - 1)
        def _():
            tbuf[c, 2, :, 128:] = jnp.zeros((chans, 128), jnp.bfloat16)

    @pl.loop(0, rows)
    def _(i):
        c = inner_first(i)
        base = hid[c] + jnp.dot(
            ws[...], raw[c + 1].reshape(2 * chans, 256), preferred_element_type=jnp.float32
        )

        @pl.when(has_prev)
        def _():
            to_next(c).wait_recv()

        @pl.when(has_next)
        def _():
            to_prev(c).wait_recv()

        mixed = jnp.dot(
            wt[...], tbuf[c].reshape(3 * chans, 256), preferred_element_type=jnp.float32
        )
        result = (base + mixed).astype(jnp.bfloat16)
        out[0, c] = result[:, :128]
        out[1, c] = result[:, 128:]

    @pl.loop(0, rows)
    def _(r):
        row_copy(r).wait_send()

        @pl.when(has_prev)
        def _():
            to_prev(r).wait_send()

        @pl.when(has_next)
        def _():
            to_next(r).wait_send()

    @pl.when(has_up)
    def _():
        own_up().wait_send()
        far_up().wait_send()
        mid_up().wait_send()

    @pl.when(has_down)
    def _():
        own_down().wait_send()
        far_down().wait_send()
        mid_down().wait_send()


def in_kernel(
    enc_feats, skip_feats, timesteps, time_first, time_second, embed_proj,
    conv_first, conv_second, temporal_weight, skip_weight,
):
    own, frames, rows, cols = enc_feats.shape
    chans = conv_second.shape[2]
    width = frames * cols
    temb = time_first.shape[1]
    n_frame, n_strip = lax.axis_size("frame"), lax.axis_size("strip")
    enc, skip = (part.transpose(1, 2, 0, 3) for part in (enc_feats, skip_feats))
    half_chans = chans // 2
    freq_table = jnp.exp(
        -math.log(10000.0) * jnp.arange(half_chans, dtype=jnp.float32) / half_chans
    )
    angle_rows = timesteps.astype(jnp.float32)[:, None] * freq_table[None, :]
    sinus = jnp.concatenate([jnp.cos(angle_rows), jnp.sin(angle_rows)], axis=1).astype(jnp.bfloat16)
    sinus = jnp.broadcast_to(sinus, (16, chans))
    bf16, f32 = jnp.bfloat16, jnp.float32
    dma = pltpu.SemaphoreType.DMA
    anywhere = pl.BlockSpec(memory_space=pl.ANY)
    inside = pl.BlockSpec(memory_space=pltpu.VMEM)
    pixels = rows * width
    result = pl.pallas_call(
        functools.partial(block_kernel, (n_frame, n_strip)),
        out_shape=jax.ShapeDtypeStruct((frames, rows, chans, cols), bf16),
        in_specs=[anywhere, anywhere, inside] + [anywhere] * 7,
        out_specs=inside,
        scratch_shapes=[
            pltpu.VMEM((rows + 2, 2, chans, width), bf16),
            pltpu.VMEM((rows + 2, 2, chans, width), bf16),
            pltpu.VMEM((rows, chans, width), f32),
            pltpu.VMEM((rows + 2, chans, width), bf16),
            pltpu.VMEM((rows, 3, chans, width), bf16),
            pltpu.VMEM((chans, 128), f32),
            pltpu.VMEM((chans, 128), f32),
            pltpu.VMEM((2, 2, chans, 128), f32),
            pltpu.VMEM((2, chans, 128), f32),
            pltpu.VMEM((chans, 128), f32),
            pltpu.VMEM((3 * chans, 6 * chans), bf16),
            pltpu.VMEM((3, 3, chans, chans), bf16),
            pltpu.VMEM((3 * chans, 3 * chans), bf16),
            pltpu.VMEM((3, chans, chans), bf16),
            pltpu.VMEM((chans, 3 * chans), bf16),
            pltpu.VMEM((chans, 2 * chans), bf16),
            pltpu.VMEM((chans, temb), bf16),
            pltpu.VMEM((temb, temb), bf16),
            pltpu.VMEM((chans, temb), bf16),
            pltpu.VMEM((5, 8, 128), f32),
            pltpu.VMEM((2, n_strip - 1, 8, 128), f32),
            pltpu.VMEM((2, n_frame - 1, 8, 128), f32),
            pltpu.VMEM((8, 128), f32),
            dma((15,)), dma((2, 2)),
            dma((rows,)), dma((rows,)),
            dma((2,)), dma((2,)), dma((2,)), dma((2,)), dma((2,)), dma((2,)),
            dma((2, rows)), dma((2, rows)),
            dma((2, n_strip - 1)), dma((2, n_strip - 1)),
            dma((2, n_frame - 1)), dma((2, n_frame - 1)),
            dma, dma,
        ],
        compiler_params=pltpu.CompilerParams(
            collective_id=0, has_side_effects=True, vmem_limit_bytes=58 * 2**20
        ),
        cost_estimate=pl.CostEstimate(
            flops=2 * pixels * chans * chans * (18 + 9 + 3 + 2),
            bytes_accessed=14 * 2**20,
            transcendentals=pixels * chans * 4,
        ),
    )(enc, skip, sinus, time_first, time_second, embed_proj.T, conv_first, conv_second, temporal_weight, skip_weight)
    return result.transpose(2, 0, 1, 3)[None]


def block(*args):
    own, frames, rows, cols = args[0].shape
    fits = (
        lax.axis_size("step") == 2
        and own % 16 == 0
        and args[7].shape[2] == 2 * own
        and (own * 4) % GROUPS == 0
        and own % (own * 4 // GROUPS) == 0
        and frames == 2
        and rows == 8
        and cols == 128
    )
    return in_kernel(*args) if fits else on_device(*args)


def solution(mesh):
    return jax.shard_map(
        block,
        mesh=mesh,
        in_specs=(
            P("step", "frame", "strip", None),
            P("step", "frame", "strip", None),
            P("step"),
            P(),
            P(),
            P(),
            P(),
            P(),
            P(),
            P(),
        ),
        out_specs=P("step", None, "frame", "strip", None),
        check_vma=False,
    )
```

```python
import functools
import math

import jax
import jax.numpy as jnp
from jax import lax
from jax.experimental import pallas as pl
from jax.experimental.pallas import tpu as pltpu
from jax.sharding import PartitionSpec as P

GROUPS = 32


norm_eps = 1e-05


def with_halo(cells, sides, width):
    for axis, dim in sides:
        count = lax.axis_size(axis)
        ends = count - 1
        head = lax.slice_in_dim(cells, 0, width, axis=dim)
        tail = lax.slice_in_dim(cells, cells.shape[dim] - width, cells.shape[dim], axis=dim)
        cells = jnp.concatenate(
            [
                lax.ppermute(tail, axis, [(i, (i + 1) % count) for i in range(ends)]),
                cells,
                lax.ppermute(head, axis, [((i + 1) % count, i) for i in range(ends)]),
            ],
            axis=dim,
        )
    return cells


def conv_taps(padded, weights):
    row_count = padded.shape[2] - 2
    col_count = padded.shape[3]
    padded_cols = jnp.pad(padded, ((0, 0), (0, 0), (0, 0), (1, 1)))
    running = jnp.zeros((weights.shape[2], padded.shape[1], row_count, col_count), jnp.float32)
    for row_off in range(3):
        for col_off in range(3):
            window = padded_cols[:, :, row_off : row_off + row_count, col_off : col_off + col_count]
            running = running + jnp.einsum(
                "oi,ifhw->ofhw",
                weights[row_off, col_off],
                window,
                preferred_element_type=jnp.float32,
            )
    return running


def channel_scales(sum_one, sum_two, groups, count_all):
    per_group = sum_one.shape[0] // groups
    mean_group = sum_one.reshape(groups, per_group).sum(axis=1) / count_all
    square_group = sum_two.reshape(groups, per_group).sum(axis=1) / count_all
    rstd_group = lax.rsqrt(square_group - mean_group * mean_group + norm_eps)
    return (jnp.repeat(mean_group, per_group), jnp.repeat(rstd_group, per_group))


def on_device(
    enc_feats,
    skip_feats,
    timesteps,
    time_first,
    time_second,
    embed_proj,
    conv_first,
    conv_second,
    temporal_weight,
    skip_weight,
):
    channels = conv_second.shape[2]
    own_chans = enc_feats.shape[0]
    frames = enc_feats.shape[1]
    row_count = enc_feats.shape[2]
    col_count = enc_feats.shape[3]
    spread = lax.axis_size("frame") * lax.axis_size("strip")
    chan_start = lax.axis_index("step") * own_chans
    stacked = jnp.stack([enc_feats, skip_feats])
    wide_feats = stacked.astype(jnp.float32)
    local_one = jnp.sum(wide_feats, axis=(2, 3, 4))
    local_two = jnp.sum(wide_feats * wide_feats, axis=(2, 3, 4))
    anchor = jnp.zeros((), jnp.int32)
    place_one = lax.dynamic_update_slice(
        jnp.zeros((2, channels), jnp.float32), local_one, (anchor, chan_start)
    )
    place_two = lax.dynamic_update_slice(
        jnp.zeros((2, channels), jnp.float32), local_two, (anchor, chan_start)
    )
    total_one, total_two = lax.psum((place_one, place_two), ("step", "frame", "strip"))
    in_count = frames * row_count * col_count * spread * (2 * channels // GROUPS)
    mean_in, rstd_in = channel_scales(
        total_one.reshape(-1), total_two.reshape(-1), GROUPS, in_count
    )
    rimmed = with_halo(stacked, (("strip", 3),), 1)
    strip_at = lax.axis_index("strip")
    strip_last = lax.axis_size("strip") - 1
    positions = jnp.arange(row_count + 2)
    row_keep = (
        ((positions > 0) | (strip_at > 0)) & ((positions < row_count + 1) | (strip_at < strip_last))
    ).astype(jnp.float32)
    pieces = lax.all_gather(rimmed, "step", axis=1, tiled=True)
    chans_here = pieces.shape[1]
    mean_rows = jnp.stack(
        [
            lax.slice_in_dim(mean_in, 0, chans_here, axis=0),
            lax.dynamic_slice_in_dim(mean_in, channels, chans_here),
        ]
    )
    rstd_rows = jnp.stack(
        [
            lax.slice_in_dim(rstd_in, 0, chans_here, axis=0),
            lax.dynamic_slice_in_dim(rstd_in, channels, chans_here),
        ]
    )
    normed = jax.nn.silu(
        (pieces.astype(jnp.float32) - mean_rows[:, :, None, None, None])
        * rstd_rows[:, :, None, None, None]
    )
    normed = normed * row_keep[None, None, None, :, None]
    act_rows = normed.astype(jnp.bfloat16).reshape(2 * chans_here, frames, row_count + 2, col_count)
    tap_weights = jnp.concatenate(
        [
            lax.slice_in_dim(conv_first, 0, chans_here, axis=3),
            lax.dynamic_slice_in_dim(conv_first, channels, chans_here, 3),
        ],
        axis=3,
    )
    skip_cols = jnp.concatenate(
        [
            lax.slice_in_dim(skip_weight, 0, chans_here, axis=1),
            lax.dynamic_slice_in_dim(skip_weight, channels, chans_here, 1),
        ],
        axis=1,
    )
    inner_rows = pieces[:, :, :, 1 : row_count + 1].reshape(
        2 * chans_here, frames, row_count, col_count
    )
    conv_part = conv_taps(act_rows, tap_weights)
    skip_part = jnp.einsum(
        "oi,ifhw->ofhw", skip_cols, inner_rows, preferred_element_type=jnp.float32
    )
    half_chans = channels // 2
    freq_table = jnp.exp(
        -math.log(10000.0) * jnp.arange(half_chans, dtype=jnp.float32) / half_chans
    )
    angle_rows = timesteps.astype(jnp.float32)[:, None] * freq_table[None, :]
    sinus_rows = jnp.concatenate([jnp.cos(angle_rows), jnp.sin(angle_rows)], axis=1).astype(
        jnp.bfloat16
    )
    embed_one = jax.nn.silu(
        jnp.dot(sinus_rows, time_first, preferred_element_type=jnp.float32)
    ).astype(jnp.bfloat16)
    embed_two = jax.nn.silu(
        jnp.dot(embed_one, time_second, preferred_element_type=jnp.float32)
    ).astype(jnp.bfloat16)
    step_embed = jnp.dot(embed_two, embed_proj, preferred_element_type=jnp.float32)
    hidden = conv_part + step_embed[0][:, None, None, None]
    hidden_one = jnp.sum(hidden, axis=(1, 2, 3))
    hidden_two = jnp.sum(hidden * hidden, axis=(1, 2, 3))
    total_hone, total_htwo = lax.psum((hidden_one, hidden_two), ("frame", "strip"))
    mid_count = frames * row_count * col_count * spread * (channels // GROUPS)
    mean_mid, rstd_mid = channel_scales(total_hone, total_htwo, GROUPS, mid_count)
    mid_act = jax.nn.silu(
        (hidden - mean_mid[:, None, None, None]) * rstd_mid[:, None, None, None]
    ).astype(jnp.bfloat16)
    mid_rim = with_halo(mid_act, (("strip", 2),), 1)
    second = conv_taps(mid_rim, conv_second)
    temporal_in = jax.nn.silu(second).astype(jnp.bfloat16)
    framed = with_halo(temporal_in, (("frame", 1),), 1)
    mixed_out = second
    for offset in range(3):
        mixed_out = mixed_out + jnp.einsum(
            "oi,ifhw->ofhw",
            temporal_weight[offset],
            framed[:, offset : offset + frames],
            preferred_element_type=jnp.float32,
        )
    decoded = (skip_part + mixed_out).astype(jnp.bfloat16)
    return decoded[None]


MESH = pl.DeviceIdType.MESH
HIGH = lax.Precision.HIGHEST


def silu(v):
    h = 0.5 * v
    return h + h * jnp.tanh(h)


def lane_dot(a, b):
    return lax.dot_general(
        a, b, (((1,), (1,)), ((), ())), precision=HIGH, preferred_element_type=jnp.float32
    )


def one_hot(shape, dim, per_group, offset):
    chan = lax.broadcasted_iota(jnp.int32, shape, dim)
    group = lax.broadcasted_iota(jnp.int32, shape, 1 - dim) - offset
    low = group * per_group
    return jnp.where((chan >= low) & (chan < low + per_group), 1.0, 0.0).astype(jnp.float32)


def pack_sums(one, two, per_group):
    count = one.shape[0]
    groups = count // per_group
    tall = jnp.dot(
        one_hot((128, count), 1, per_group, 0), one, precision=HIGH, preferred_element_type=jnp.float32
    ) + jnp.dot(
        one_hot((128, count), 1, per_group, groups), two, precision=HIGH, preferred_element_type=jnp.float32
    )
    return lane_dot(jnp.ones((8, 128), jnp.float32), tall)


def columns_of(total, count, per_group, entries):
    groups = count // per_group
    mean = lane_dot(one_hot((count, 128), 0, per_group, 0), total)[:, :1] / entries
    square = lane_dot(one_hot((count, 128), 0, per_group, groups), total)[:, :1] / entries
    rstd = lax.rsqrt(square - mean * mean + norm_eps)
    return jnp.broadcast_to(mean, (count, 128)), jnp.broadcast_to(rstd, (count, 128))


def push(src, dst, send, recv, axis, target):
    return pltpu.make_async_remote_copy(
        src_ref=src, dst_ref=dst, send_sem=send, recv_sem=recv,
        device_id={axis: target}, device_id_type=MESH,
    )


def peers_of(n_frame, n_strip):
    frame, strip = lax.axis_index("frame"), lax.axis_index("strip")
    return [
        {"frame": lax.rem(frame + df, n_frame), "strip": lax.rem(strip + ds, n_strip)}
        for df in range(n_frame)
        for ds in range(n_strip)
        if df or ds
    ]


def send_all(src, slots, send, recv, peers):
    copies = [
        pltpu.make_async_remote_copy(
            src_ref=src, dst_ref=slots.at[d], send_sem=send.at[d], recv_sem=recv.at[d],
            device_id=peer, device_id_type=MESH,
        )
        for d, peer in enumerate(peers)
    ]
    for copy in copies:
        copy.start()
    return copies


def add_all(src, slots, copies):
    total = src[...]
    for d, copy in enumerate(copies):
        copy.wait_recv()
        total = total + slots[d]
    return total


def join_taps(found, chans, f):
    lanes = slice(f * 128, f * 128 + 128)
    lane = lax.broadcasted_iota(jnp.int32, (chans, 128), 1)
    before = pltpu.roll(found[:chans, lanes], 1, 1)
    after = pltpu.roll(found[2 * chans :, lanes], 127, 1)
    return (
        found[chans : 2 * chans, lanes]
        + jnp.where(lane == 0, 0.0, before)
        + jnp.where(lane == 127, 0.0, after)
    )


def block_kernel(
    sizes,
    enc, skip, sinus, first_h, second_h, proj_h, conv1_h, conv2_h, temp_h, skip_h,
    out,
    raw, act, hid, skipped, act2, tbuf, acc1, acc2, cols_in, cols_mid, emb,
    w1, w2raw, w2, wtraw, wt, ws, tf, ts, ep,
    stats, slots, slot_step,
    wsem, own_sem, x_send, x_recv, h_send, h_recv, g_send, g_recv, m_send, m_recv,
    t_send, t_recv, s_send, s_recv, sx_send, sx_recv,
):
    n_frame, n_strip = sizes
    rows, own = enc.shape[1], enc.shape[2]
    chans = 2 * own
    last = rows - 1
    step, frame, strip = (lax.axis_index(a) for a in ("step", "frame", "strip"))
    partner = 1 - step
    mine = pl.ds(pl.multiple_of(step * own, 16), own)
    theirs = pl.ds(pl.multiple_of(partner * own, 16), own)

    loads = [pltpu.make_async_copy(conv1_h, w1, wsem.at[0])]
    small = [
        pltpu.make_async_copy(src, dst, wsem.at[9 + i])
        for i, (src, dst) in enumerate(
            ((first_h, tf), (second_h, ts), (proj_h, ep), (conv2_h, w2raw), (temp_h, wtraw), (skip_h, ws))
        )
    ]
    keeps = [
        pltpu.make_async_copy(
            source.at[f], raw.at[pl.ds(1, rows), h, mine, pl.ds(f * 128, 128)], own_sem.at[h, f]
        )
        for h, source in enumerate((enc, skip))
        for f in range(2)
    ]
    for keep in keeps:
        keep.start()

    barrier = pltpu.get_barrier_semaphore()
    peers = peers_of(n_frame, n_strip)
    for peer in peers + [{"step": partner}]:
        pl.semaphore_signal(barrier, inc=1, device_id=peer, device_id_type=MESH)
    pl.semaphore_wait(barrier, len(peers) + 1)
    for keep in keeps:
        keep.wait()

    def row_copy(r):
        return push(raw.at[r + 1, :, mine, :], raw.at[r + 1, :, mine, :], x_send.at[r], x_recv.at[r], "step", partner)

    def own_up():
        return push(raw.at[1, :, mine, :], raw.at[rows + 1, :, mine, :], h_send.at[1], h_recv.at[1], "strip", strip - 1)

    def own_down():
        return push(raw.at[rows, :, mine, :], raw.at[0, :, mine, :], h_send.at[0], h_recv.at[0], "strip", strip + 1)

    def far_up():
        return push(
            raw.at[1, :, theirs, :], raw.at[rows + 1, :, theirs, :], g_send.at[1], g_recv.at[1], "strip", strip - 1
        )

    def far_down():
        return push(
            raw.at[rows, :, theirs, :], raw.at[0, :, theirs, :], g_send.at[0], g_recv.at[0], "strip", strip + 1
        )

    has_up, has_down = strip > 0, strip < n_strip - 1
    for r in (0, last):
        row_copy(r).start()
    pl.when(has_up)(lambda: own_up().start())
    pl.when(has_down)(lambda: own_down().start())

    @pl.loop(1, last)
    def _(r):
        row_copy(r).start()

    for load in loads + small:
        load.start()

    acc1[...] = jnp.zeros_like(acc1)
    acc2[...] = jnp.zeros_like(acc2)

    @pl.loop(0, rows)
    def _(r):
        for h in range(2):
            wide = raw[r + 1, h, mine, :].astype(jnp.float32)
            a, b = wide[:, :128], wide[:, 128:]
            at = pl.ds(h * own, own)
            acc1[at, :] = acc1[at, :] + (a + b)
            acc2[at, :] = acc2[at, :] + (a * a + b * b)

    per_in = 2 * chans // GROUPS
    stats[0] = pack_sums(acc1[...], acc2[...], per_in)
    sent = send_all(stats.at[0], slots.at[0], s_send.at[0], s_recv.at[0], peers)
    stats[1] = add_all(stats.at[0], slots.at[0], sent)
    swap = push(stats.at[1], slot_step, sx_send, sx_recv, "step", partner)
    swap.start()
    entries = 2 * rows * 128 * n_frame * n_strip
    in_entries = float(entries * per_in)

    def set_cols(total, at):
        mean, rstd = columns_of(total, chans, per_in, in_entries)
        for h in range(2):
            cols_in[0, h, at, :] = mean[h * own : (h + 1) * own]
            cols_in[1, h, at, :] = rstd[h * own : (h + 1) * own]

    set_cols(stats[1], mine)

    def make_act(r, at):
        for h in range(2):
            mean, rstd = cols_in[0, h, at, :], cols_in[1, h, at, :]
            for f in range(2):
                lanes = pl.ds(f * 128, 128)
                value = silu((raw[r, h, at, lanes].astype(jnp.float32) - mean) * rstd)
                act[r, h, at, lanes] = value.astype(jnp.bfloat16)

    @pl.loop(1, rows + 1)
    def _(r):
        make_act(r, mine)

    @pl.when(has_up)
    def _():
        own_down().wait_recv()
        make_act(0, mine)

    @pl.when(has_down)
    def _():
        own_up().wait_recv()
        make_act(rows + 1, mine)

    swap.wait()
    set_cols(slot_step[...], theirs)

    for load in small:
        load.wait()
    one = silu(jnp.dot(
        jnp.broadcast_to(sinus[...].astype(jnp.float32), (16, chans)).astype(jnp.bfloat16), tf[...], preferred_element_type=jnp.float32)).astype(jnp.bfloat16)
    two = silu(jnp.dot(one, ts[...], preferred_element_type=jnp.float32)).astype(jnp.bfloat16)
    embed = lax.dot_general(
        ep[...], two, (((1,), (1,)), ((), ())), preferred_element_type=jnp.float32
    )
    emb[...] = jnp.broadcast_to(embed[:, :1], (chans, 128))
    for t in range(9):
        dy, dx = t // 3, t % 3
        w2[dx * chans : (dx + 1) * chans, dy * chans : (dy + 1) * chans] = w2raw[dy, dx]
    for t in range(3):
        wt[:, t * chans : (t + 1) * chans] = wtraw[t]
    for load in loads:
        load.wait()

    start_value = jnp.concatenate([emb[...], emb[...]], axis=1)

    @pl.loop(0, rows + 4)
    def _(r):
        hid[r] = start_value

    def add_taps(r, offsets):
        image_row = act[r].reshape(2 * chans, 256)
        for dy in offsets:
            found = jnp.dot(
                w1[dy].reshape(3 * chans, 2 * chans), image_row, preferred_element_type=jnp.float32
            )
            for f in range(2):
                lanes = pl.ds(f * 128, 128)
                hid[r - dy + 2, :, lanes] = hid[r - dy + 2, :, lanes] + join_taps(found, chans, f)

    def add_skip(r):
        skipped[r] = jnp.dot(
            ws[...], raw[r + 1].reshape(2 * chans, 256), preferred_element_type=jnp.float32
        )

    def arrival(i):
        later = (i + rows - 2) // rows
        return (i - 1) * later + last * i * (1 - later)

    @pl.loop(0, rows)
    def _(i):
        r = arrival(i)

        @pl.when(i > 0)
        def _():
            add_skip(arrival(i - 1))

        row_copy(r).wait_recv()

        @pl.when((i == 0) & has_up)
        def _():
            far_up().start()

        @pl.when((i == 1) & has_down)
        def _():
            far_down().start()

        make_act(r + 1, theirs)
        add_taps(r + 1, (0, 1, 2))

        @pl.when((i == rows - 3) & has_up)
        def _():
            far_down().wait_recv()
            make_act(0, theirs)
            add_taps(0, (0,))

        @pl.when((i == rows - 3) & has_down)
        def _():
            far_up().wait_recv()
            make_act(rows + 1, theirs)
            add_taps(rows + 1, (2,))

    acc1[...] = jnp.zeros_like(acc1)
    acc2[...] = jnp.zeros_like(acc2)

    @pl.loop(0, rows)
    def _(c):
        a, b = hid[c + 2, :, :128], hid[c + 2, :, 128:]
        acc1[...] = acc1[...] + (a + b)
        acc2[...] = acc2[...] + (a * a + b * b)

    per_mid = chans // GROUPS
    stats[2] = pack_sums(acc1[...], acc2[...], per_mid)
    sent_mid = send_all(stats.at[2], slots.at[1], s_send.at[1], s_recv.at[1], peers)
    add_skip(last - 1)
    total = add_all(stats.at[2], slots.at[1], sent_mid)
    mean, rstd = columns_of(total, chans, per_mid, float(entries * per_mid))
    cols_mid[0] = mean
    cols_mid[1] = rstd

    def mid_row(r):
        for f in range(2):
            lanes = pl.ds(f * 128, 128)
            value = silu((hid[r + 2, :, lanes] - cols_mid[0]) * cols_mid[1])
            act2[r + 1, :, lanes] = value.astype(jnp.bfloat16)

    def mid_up():
        return push(act2.at[1], act2.at[rows + 1], m_send.at[1], m_recv.at[1], "strip", strip - 1)

    def mid_down():
        return push(act2.at[rows], act2.at[0], m_send.at[0], m_recv.at[0], "strip", strip + 1)

    mid_row(0)
    pl.when(has_up)(lambda: mid_up().start())
    mid_row(last)
    pl.when(has_down)(lambda: mid_down().start())

    @pl.loop(1, last)
    def _(r):
        mid_row(r)

    has_prev, has_next = frame > 0, frame < n_frame - 1

    def to_prev(c):
        return push(
            tbuf.at[c, 1, :, pl.ds(0, 128)], tbuf.at[c, 2, :, pl.ds(128, 128)],
            t_send.at[0, c], t_recv.at[0, c], "frame", frame - 1,
        )

    def to_next(c):
        return push(
            tbuf.at[c, 1, :, pl.ds(128, 128)], tbuf.at[c, 0, :, pl.ds(0, 128)],
            t_send.at[1, c], t_recv.at[1, c], "frame", frame + 1,
        )

    def inner_first(i):
        tail = i // (rows - 2)
        return (i + 1) * (1 - tail) + (i - (rows - 2)) * last * tail

    @pl.loop(0, rows)
    def _(i):
        c = inner_first(i)

        @pl.when((i == rows - 2) & has_up)
        def _():
            mid_down().wait_recv()

        @pl.when((i == rows - 2) & has_down)
        def _():
            mid_up().wait_recv()

        @pl.when((i == rows - 2) & (strip == 0))
        def _():
            act2[0] = jnp.zeros(act2.shape[1:], jnp.bfloat16)

        @pl.when((i == rows - 2) & (strip == n_strip - 1))
        def _():
            act2[rows + 1] = jnp.zeros(act2.shape[1:], jnp.bfloat16)

        window = act2[pl.ds(c, 3)].reshape(3 * chans, 256)
        found = jnp.dot(w2[...], window, preferred_element_type=jnp.float32)
        for f in range(2):
            lanes = pl.ds(f * 128, 128)
            second = join_taps(found, chans, f)
            hid[c, :, lanes] = second
            inner = silu(second).astype(jnp.bfloat16)
            tbuf[c, 1, :, lanes] = inner
            tbuf[c, 2 * f, :, pl.ds(128 - f * 128, 128)] = inner

        @pl.when(has_prev)
        def _():
            to_prev(c).start()

        @pl.when(has_next)
        def _():
            to_next(c).start()

        @pl.when(frame == 0)
        def _():
            tbuf[c, 0, :, :128] = jnp.zeros((chans, 128), jnp.bfloat16)

        @pl.when(frame == n_frame - 1)
        def _():
            tbuf[c, 2, :, 128:] = jnp.zeros((chans, 128), jnp.bfloat16)

    @pl.loop(0, rows)
    def _(i):
        c = inner_first(i)
        base = hid[c] + skipped[c]

        @pl.when(has_prev)
        def _():
            to_next(c).wait_recv()

        @pl.when(has_next)
        def _():
            to_prev(c).wait_recv()

        mixed = jnp.dot(
            wt[...], tbuf[c].reshape(3 * chans, 256), preferred_element_type=jnp.float32
        )
        result = (base + mixed).astype(jnp.bfloat16)
        out[0, c] = result[:, :128]
        out[1, c] = result[:, 128:]

    @pl.loop(0, rows)
    def _(r):
        row_copy(r).wait_send()

        @pl.when(has_prev)
        def _():
            to_prev(r).wait_send()

        @pl.when(has_next)
        def _():
            to_next(r).wait_send()

    for copy in sent + sent_mid:
        copy.wait_send()

    @pl.when(has_up)
    def _():
        own_up().wait_send()
        far_up().wait_send()
        mid_up().wait_send()

    @pl.when(has_down)
    def _():
        own_down().wait_send()
        far_down().wait_send()
        mid_down().wait_send()


def in_kernel(
    enc_feats, skip_feats, timesteps, time_first, time_second, embed_proj,
    conv_first, conv_second, temporal_weight, skip_weight,
):
    own, frames, rows, cols = enc_feats.shape
    chans = conv_second.shape[2]
    width = frames * cols
    temb = time_first.shape[1]
    n_frame, n_strip = lax.axis_size("frame"), lax.axis_size("strip")
    enc, skip = (part.transpose(1, 2, 0, 3) for part in (enc_feats, skip_feats))
    n_peer = n_frame * n_strip - 1
    half_chans = chans // 2
    freq_table = jnp.exp(
        -math.log(10000.0) * jnp.arange(half_chans, dtype=jnp.float32) / half_chans
    )
    angle_rows = timesteps.astype(jnp.float32)[:, None] * freq_table[None, :]
    sinus = jnp.concatenate([jnp.cos(angle_rows), jnp.sin(angle_rows)], axis=1).astype(jnp.bfloat16)
    bf16, f32 = jnp.bfloat16, jnp.float32
    dma = pltpu.SemaphoreType.DMA
    anywhere = pl.BlockSpec(memory_space=pl.ANY)
    inside = pl.BlockSpec(memory_space=pltpu.VMEM)
    pixels = rows * width
    result = pl.pallas_call(
        functools.partial(block_kernel, (n_frame, n_strip)),
        out_shape=jax.ShapeDtypeStruct((frames, rows, chans, cols), bf16),
        in_specs=[anywhere, anywhere, inside] + [anywhere] * 7,
        out_specs=inside,
        scratch_shapes=[
            pltpu.VMEM((rows + 2, 2, chans, width), bf16),
            pltpu.VMEM((rows + 2, 2, chans, width), bf16),
            pltpu.VMEM((rows + 4, chans, width), f32),
            pltpu.VMEM((rows, chans, width), f32),
            pltpu.VMEM((rows + 2, chans, width), bf16),
            pltpu.VMEM((rows, 3, chans, width), bf16),
            pltpu.VMEM((chans, 128), f32),
            pltpu.VMEM((chans, 128), f32),
            pltpu.VMEM((2, 2, chans, 128), f32),
            pltpu.VMEM((2, chans, 128), f32),
            pltpu.VMEM((chans, 128), f32),
            pltpu.VMEM((3, 3, chans, 2 * chans), bf16),
            pltpu.VMEM((3, 3, chans, chans), bf16),
            pltpu.VMEM((3 * chans, 3 * chans), bf16),
            pltpu.VMEM((3, chans, chans), bf16),
            pltpu.VMEM((chans, 3 * chans), bf16),
            pltpu.VMEM((chans, 2 * chans), bf16),
            pltpu.VMEM((chans, temb), bf16),
            pltpu.VMEM((temb, temb), bf16),
            pltpu.VMEM((chans, temb), bf16),
            pltpu.VMEM((3, 8, 128), f32),
            pltpu.VMEM((2, n_peer, 8, 128), f32),
            pltpu.VMEM((8, 128), f32),
            dma((15,)), dma((2, 2)),
            dma((rows,)), dma((rows,)),
            dma((2,)), dma((2,)), dma((2,)), dma((2,)), dma((2,)), dma((2,)),
            dma((2, rows)), dma((2, rows)),
            dma((2, n_peer)), dma((2, n_peer)),
            dma, dma,
        ],
        compiler_params=pltpu.CompilerParams(
            collective_id=0, has_side_effects=True, vmem_limit_bytes=58 * 2**20
        ),
        cost_estimate=pl.CostEstimate(
            flops=2 * pixels * chans * chans * (18 + 9 + 3 + 2),
            bytes_accessed=14 * 2**20,
            transcendentals=pixels * chans * 4,
        ),
    )(enc, skip, sinus, time_first, time_second, embed_proj.T, conv_first, conv_second, temporal_weight, skip_weight)
    return result.transpose(2, 0, 1, 3)[None]


def block(*args):
    own, frames, rows, cols = args[0].shape
    fits = (
        lax.axis_size("step") == 2
        and own % 16 == 0
        and args[7].shape[2] == 2 * own
        and (own * 4) % GROUPS == 0
        and own % (own * 4 // GROUPS) == 0
        and frames == 2
        and rows == 8
        and cols == 128
    )
    return in_kernel(*args) if fits else on_device(*args)


def solution(mesh):
    return jax.shard_map(
        block,
        mesh=mesh,
        in_specs=(
            P("step", "frame", "strip", None),
            P("step", "frame", "strip", None),
            P("step"),
            P(),
            P(),
            P(),
            P(),
            P(),
            P(),
            P(),
        ),
        out_specs=P("step", None, "frame", "strip", None),
        check_vma=False,
    )
```

```python
import functools
import math

import jax
import jax.numpy as jnp
from jax import lax
from jax.experimental import pallas as pl
from jax.experimental.pallas import tpu as pltpu
from jax.sharding import PartitionSpec as P

GROUPS = 32


norm_eps = 1e-05


def with_halo(cells, sides, width):
    for axis, dim in sides:
        count = lax.axis_size(axis)
        ends = count - 1
        head = lax.slice_in_dim(cells, 0, width, axis=dim)
        tail = lax.slice_in_dim(cells, cells.shape[dim] - width, cells.shape[dim], axis=dim)
        cells = jnp.concatenate(
            [
                lax.ppermute(tail, axis, [(i, (i + 1) % count) for i in range(ends)]),
                cells,
                lax.ppermute(head, axis, [((i + 1) % count, i) for i in range(ends)]),
            ],
            axis=dim,
        )
    return cells


def conv_taps(padded, weights):
    row_count = padded.shape[2] - 2
    col_count = padded.shape[3]
    padded_cols = jnp.pad(padded, ((0, 0), (0, 0), (0, 0), (1, 1)))
    running = jnp.zeros((weights.shape[2], padded.shape[1], row_count, col_count), jnp.float32)
    for row_off in range(3):
        for col_off in range(3):
            window = padded_cols[:, :, row_off : row_off + row_count, col_off : col_off + col_count]
            running = running + jnp.einsum(
                "oi,ifhw->ofhw",
                weights[row_off, col_off],
                window,
                preferred_element_type=jnp.float32,
            )
    return running


def channel_scales(sum_one, sum_two, groups, count_all):
    per_group = sum_one.shape[0] // groups
    mean_group = sum_one.reshape(groups, per_group).sum(axis=1) / count_all
    square_group = sum_two.reshape(groups, per_group).sum(axis=1) / count_all
    rstd_group = lax.rsqrt(square_group - mean_group * mean_group + norm_eps)
    return (jnp.repeat(mean_group, per_group), jnp.repeat(rstd_group, per_group))


def on_device(
    enc_feats,
    skip_feats,
    timesteps,
    time_first,
    time_second,
    embed_proj,
    conv_first,
    conv_second,
    temporal_weight,
    skip_weight,
):
    channels = conv_second.shape[2]
    own_chans = enc_feats.shape[0]
    frames = enc_feats.shape[1]
    row_count = enc_feats.shape[2]
    col_count = enc_feats.shape[3]
    spread = lax.axis_size("frame") * lax.axis_size("strip")
    chan_start = lax.axis_index("step") * own_chans
    stacked = jnp.stack([enc_feats, skip_feats])
    wide_feats = stacked.astype(jnp.float32)
    local_one = jnp.sum(wide_feats, axis=(2, 3, 4))
    local_two = jnp.sum(wide_feats * wide_feats, axis=(2, 3, 4))
    anchor = jnp.zeros((), jnp.int32)
    place_one = lax.dynamic_update_slice(
        jnp.zeros((2, channels), jnp.float32), local_one, (anchor, chan_start)
    )
    place_two = lax.dynamic_update_slice(
        jnp.zeros((2, channels), jnp.float32), local_two, (anchor, chan_start)
    )
    total_one, total_two = lax.psum((place_one, place_two), ("step", "frame", "strip"))
    in_count = frames * row_count * col_count * spread * (2 * channels // GROUPS)
    mean_in, rstd_in = channel_scales(
        total_one.reshape(-1), total_two.reshape(-1), GROUPS, in_count
    )
    rimmed = with_halo(stacked, (("strip", 3),), 1)
    strip_at = lax.axis_index("strip")
    strip_last = lax.axis_size("strip") - 1
    positions = jnp.arange(row_count + 2)
    row_keep = (
        ((positions > 0) | (strip_at > 0)) & ((positions < row_count + 1) | (strip_at < strip_last))
    ).astype(jnp.float32)
    pieces = lax.all_gather(rimmed, "step", axis=1, tiled=True)
    chans_here = pieces.shape[1]
    mean_rows = jnp.stack(
        [
            lax.slice_in_dim(mean_in, 0, chans_here, axis=0),
            lax.dynamic_slice_in_dim(mean_in, channels, chans_here),
        ]
    )
    rstd_rows = jnp.stack(
        [
            lax.slice_in_dim(rstd_in, 0, chans_here, axis=0),
            lax.dynamic_slice_in_dim(rstd_in, channels, chans_here),
        ]
    )
    normed = jax.nn.silu(
        (pieces.astype(jnp.float32) - mean_rows[:, :, None, None, None])
        * rstd_rows[:, :, None, None, None]
    )
    normed = normed * row_keep[None, None, None, :, None]
    act_rows = normed.astype(jnp.bfloat16).reshape(2 * chans_here, frames, row_count + 2, col_count)
    tap_weights = jnp.concatenate(
        [
            lax.slice_in_dim(conv_first, 0, chans_here, axis=3),
            lax.dynamic_slice_in_dim(conv_first, channels, chans_here, 3),
        ],
        axis=3,
    )
    skip_cols = jnp.concatenate(
        [
            lax.slice_in_dim(skip_weight, 0, chans_here, axis=1),
            lax.dynamic_slice_in_dim(skip_weight, channels, chans_here, 1),
        ],
        axis=1,
    )
    inner_rows = pieces[:, :, :, 1 : row_count + 1].reshape(
        2 * chans_here, frames, row_count, col_count
    )
    conv_part = conv_taps(act_rows, tap_weights)
    skip_part = jnp.einsum(
        "oi,ifhw->ofhw", skip_cols, inner_rows, preferred_element_type=jnp.float32
    )
    half_chans = channels // 2
    freq_table = jnp.exp(
        -math.log(10000.0) * jnp.arange(half_chans, dtype=jnp.float32) / half_chans
    )
    angle_rows = timesteps.astype(jnp.float32)[:, None] * freq_table[None, :]
    sinus_rows = jnp.concatenate([jnp.cos(angle_rows), jnp.sin(angle_rows)], axis=1).astype(
        jnp.bfloat16
    )
    embed_one = jax.nn.silu(
        jnp.dot(sinus_rows, time_first, preferred_element_type=jnp.float32)
    ).astype(jnp.bfloat16)
    embed_two = jax.nn.silu(
        jnp.dot(embed_one, time_second, preferred_element_type=jnp.float32)
    ).astype(jnp.bfloat16)
    step_embed = jnp.dot(embed_two, embed_proj, preferred_element_type=jnp.float32)
    hidden = conv_part + step_embed[0][:, None, None, None]
    hidden_one = jnp.sum(hidden, axis=(1, 2, 3))
    hidden_two = jnp.sum(hidden * hidden, axis=(1, 2, 3))
    total_hone, total_htwo = lax.psum((hidden_one, hidden_two), ("frame", "strip"))
    mid_count = frames * row_count * col_count * spread * (channels // GROUPS)
    mean_mid, rstd_mid = channel_scales(total_hone, total_htwo, GROUPS, mid_count)
    mid_act = jax.nn.silu(
        (hidden - mean_mid[:, None, None, None]) * rstd_mid[:, None, None, None]
    ).astype(jnp.bfloat16)
    mid_rim = with_halo(mid_act, (("strip", 2),), 1)
    second = conv_taps(mid_rim, conv_second)
    temporal_in = jax.nn.silu(second).astype(jnp.bfloat16)
    framed = with_halo(temporal_in, (("frame", 1),), 1)
    mixed_out = second
    for offset in range(3):
        mixed_out = mixed_out + jnp.einsum(
            "oi,ifhw->ofhw",
            temporal_weight[offset],
            framed[:, offset : offset + frames],
            preferred_element_type=jnp.float32,
        )
    decoded = (skip_part + mixed_out).astype(jnp.bfloat16)
    return decoded[None]


MESH = pl.DeviceIdType.MESH
HIGH = lax.Precision.HIGHEST


def silu(v):
    h = 0.5 * v
    return h + h * jnp.tanh(h)


def lane_dot(a, b):
    return lax.dot_general(
        a, b, (((1,), (1,)), ((), ())), precision=HIGH, preferred_element_type=jnp.float32
    )


def one_hot(shape, dim, per_group, offset):
    chan = lax.broadcasted_iota(jnp.int32, shape, dim)
    group = lax.broadcasted_iota(jnp.int32, shape, 1 - dim) - offset
    low = group * per_group
    return jnp.where((chan >= low) & (chan < low + per_group), 1.0, 0.0).astype(jnp.float32)


def pack_sums(one, two, per_group):
    count = one.shape[0]
    groups = count // per_group
    tall = jnp.dot(
        one_hot((128, count), 1, per_group, 0), one, precision=HIGH, preferred_element_type=jnp.float32
    ) + jnp.dot(
        one_hot((128, count), 1, per_group, groups), two, precision=HIGH, preferred_element_type=jnp.float32
    )
    return lane_dot(jnp.ones((8, 128), jnp.float32), tall)


def columns_of(total, count, per_group, entries):
    groups = count // per_group
    mean = lane_dot(one_hot((count, 128), 0, per_group, 0), total)[:, :1] / entries
    square = lane_dot(one_hot((count, 128), 0, per_group, groups), total)[:, :1] / entries
    rstd = lax.rsqrt(square - mean * mean + norm_eps)
    return jnp.broadcast_to(mean, (count, 128)), jnp.broadcast_to(rstd, (count, 128))


def push(src, dst, send, recv, axis, target):
    return pltpu.make_async_remote_copy(
        src_ref=src, dst_ref=dst, send_sem=send, recv_sem=recv,
        device_id={axis: target}, device_id_type=MESH,
    )


def peers_of(n_frame, n_strip):
    frame, strip = lax.axis_index("frame"), lax.axis_index("strip")
    return [
        {"frame": lax.rem(frame + df, n_frame), "strip": lax.rem(strip + ds, n_strip)}
        for df in range(n_frame)
        for ds in range(n_strip)
        if df or ds
    ]


def send_all(src, slots, send, recv, peers):
    copies = [
        pltpu.make_async_remote_copy(
            src_ref=src, dst_ref=slots.at[d], send_sem=send.at[d], recv_sem=recv.at[d],
            device_id=peer, device_id_type=MESH,
        )
        for d, peer in enumerate(peers)
    ]
    for copy in copies:
        copy.start()
    return copies


def add_all(src, slots, copies):
    total = src[...]
    for d, copy in enumerate(copies):
        copy.wait_recv()
        total = total + slots[d]
    return total


def join_taps(found, chans, f):
    lanes = slice(f * 128, f * 128 + 128)
    lane = lax.broadcasted_iota(jnp.int32, (chans, 128), 1)
    before = pltpu.roll(found[:chans, lanes], 1, 1)
    after = pltpu.roll(found[2 * chans :, lanes], 127, 1)
    return (
        found[chans : 2 * chans, lanes]
        + jnp.where(lane == 0, 0.0, before)
        + jnp.where(lane == 127, 0.0, after)
    )


def block_kernel(
    sizes,
    enc, skip, sinus, first_h, second_h, proj_h, conv1_h, conv2_h, temp_h, skip_h,
    out,
    raw, act, hid, skipped, act2, tbuf, acc1, acc2, cols_in, cols_mid, emb,
    w1, w2raw, w2, wtraw, wt, ws, tf, ts, ep,
    stats, slots, slot_step,
    wsem, own_sem, x_send, x_recv, h_send, h_recv, g_send, g_recv, m_send, m_recv,
    t_send, t_recv, s_send, s_recv, sx_send, sx_recv,
):
    n_frame, n_strip = sizes
    rows, own = enc.shape[1], enc.shape[2]
    chans = 2 * own
    last = rows - 1
    step, frame, strip = (lax.axis_index(a) for a in ("step", "frame", "strip"))
    partner = 1 - step
    mine = pl.ds(pl.multiple_of(step * own, 16), own)
    theirs = pl.ds(pl.multiple_of(partner * own, 16), own)

    loads = [
        pltpu.make_async_copy(
            conv1_h.at[t // 3, t % 3],
            w1.at[pl.ds(t % 3 * chans, chans), pl.ds(t // 3 * 2 * chans, 2 * chans)],
            wsem.at[t],
        )
        for t in range(9)
    ]
    small = [
        pltpu.make_async_copy(src, dst, wsem.at[9 + i])
        for i, (src, dst) in enumerate(
            ((first_h, tf), (second_h, ts), (proj_h, ep), (conv2_h, w2raw), (temp_h, wtraw), (skip_h, ws))
        )
    ]
    keeps = [
        pltpu.make_async_copy(
            source.at[f], raw.at[pl.ds(1, rows), h, mine, pl.ds(f * 128, 128)], own_sem.at[h, f]
        )
        for h, source in enumerate((enc, skip))
        for f in range(2)
    ]
    for keep in keeps:
        keep.start()

    barrier = pltpu.get_barrier_semaphore()
    peers = peers_of(n_frame, n_strip)
    for peer in peers + [{"step": partner}]:
        pl.semaphore_signal(barrier, inc=1, device_id=peer, device_id_type=MESH)
    pl.semaphore_wait(barrier, len(peers) + 1)
    for keep in keeps:
        keep.wait()

    def row_copy(r):
        return push(raw.at[r + 1, :, mine, :], raw.at[r + 1, :, mine, :], x_send.at[r], x_recv.at[r], "step", partner)

    def own_up():
        return push(raw.at[1, :, mine, :], raw.at[rows + 1, :, mine, :], h_send.at[1], h_recv.at[1], "strip", strip - 1)

    def own_down():
        return push(raw.at[rows, :, mine, :], raw.at[0, :, mine, :], h_send.at[0], h_recv.at[0], "strip", strip + 1)

    def far_up():
        return push(
            raw.at[1, :, theirs, :], raw.at[rows + 1, :, theirs, :], g_send.at[1], g_recv.at[1], "strip", strip - 1
        )

    def far_down():
        return push(
            raw.at[rows, :, theirs, :], raw.at[0, :, theirs, :], g_send.at[0], g_recv.at[0], "strip", strip + 1
        )

    has_up, has_down = strip > 0, strip < n_strip - 1
    for r in (0, last):
        row_copy(r).start()
    pl.when(has_up)(lambda: own_up().start())
    pl.when(has_down)(lambda: own_down().start())

    @pl.loop(1, last)
    def _(r):
        row_copy(r).start()

    for load in loads + small:
        load.start()

    acc1[...] = jnp.zeros_like(acc1)
    acc2[...] = jnp.zeros_like(acc2)

    @pl.loop(0, rows)
    def _(r):
        for h in range(2):
            wide = raw[r + 1, h, mine, :].astype(jnp.float32)
            a, b = wide[:, :128], wide[:, 128:]
            at = pl.ds(h * own, own)
            acc1[at, :] = acc1[at, :] + (a + b)
            acc2[at, :] = acc2[at, :] + (a * a + b * b)

    per_in = 2 * chans // GROUPS
    stats[0] = pack_sums(acc1[...], acc2[...], per_in)
    sent = send_all(stats.at[0], slots.at[0], s_send.at[0], s_recv.at[0], peers)
    stats[1] = add_all(stats.at[0], slots.at[0], sent)
    swap = push(stats.at[1], slot_step, sx_send, sx_recv, "step", partner)
    swap.start()
    entries = 2 * rows * 128 * n_frame * n_strip
    in_entries = float(entries * per_in)

    def set_cols(total, at):
        mean, rstd = columns_of(total, chans, per_in, in_entries)
        for h in range(2):
            cols_in[0, h, at, :] = mean[h * own : (h + 1) * own]
            cols_in[1, h, at, :] = rstd[h * own : (h + 1) * own]

    set_cols(stats[1], mine)

    def make_act(r, at):
        for h in range(2):
            mean, rstd = cols_in[0, h, at, :], cols_in[1, h, at, :]
            for f in range(2):
                lanes = pl.ds(f * 128, 128)
                value = silu((raw[r, h, at, lanes].astype(jnp.float32) - mean) * rstd)
                act[r, h, at, lanes] = value.astype(jnp.bfloat16)

    @pl.loop(1, rows + 1)
    def _(r):
        make_act(r, mine)

    @pl.when(has_up)
    def _():
        own_down().wait_recv()
        make_act(0, mine)

    @pl.when(has_down)
    def _():
        own_up().wait_recv()
        make_act(rows + 1, mine)

    @pl.when(strip == 0)
    def _():
        act[0] = jnp.zeros(act.shape[1:], jnp.bfloat16)
        act2[0] = jnp.zeros(act2.shape[1:], jnp.bfloat16)

    @pl.when(strip == n_strip - 1)
    def _():
        act[rows + 1] = jnp.zeros(act.shape[1:], jnp.bfloat16)
        act2[rows + 1] = jnp.zeros(act2.shape[1:], jnp.bfloat16)

    swap.wait()
    set_cols(slot_step[...], theirs)

    for load in small:
        load.wait()
    one = silu(jnp.dot(
        jnp.broadcast_to(sinus[...].astype(jnp.float32), (16, chans)).astype(jnp.bfloat16), tf[...], preferred_element_type=jnp.float32)).astype(jnp.bfloat16)
    two = silu(jnp.dot(one, ts[...], preferred_element_type=jnp.float32)).astype(jnp.bfloat16)
    embed = lax.dot_general(
        ep[...], two, (((1,), (1,)), ((), ())), preferred_element_type=jnp.float32
    )
    emb[...] = jnp.broadcast_to(embed[:, :1], (chans, 128))
    for t in range(9):
        dy, dx = t // 3, t % 3
        w2[dx * chans : (dx + 1) * chans, dy * chans : (dy + 1) * chans] = w2raw[dy, dx]
    for t in range(3):
        wt[:, t * chans : (t + 1) * chans] = wtraw[t]
    for load in loads:
        load.wait()

    def arrive(r):
        row_copy(r).wait_recv()

        @pl.when((r == 0) & has_up)
        def _():
            far_up().start()

        @pl.when((r == last) & has_down)
        def _():
            far_down().start()

        make_act(r + 1, theirs)

    def pair_dot(weights, first, second):
        return jnp.dot(
            weights[...], jnp.concatenate([first, second], axis=1), preferred_element_type=jnp.float32
        )

    acc1[...] = jnp.zeros_like(acc1)
    acc2[...] = jnp.zeros_like(acc2)

    @pl.loop(0, 4)
    def _(i):
        later = (i + 2) // 4
        arrive((i - 1) * later + last * i * (1 - later))

    @pl.when(has_up)
    def _():
        far_down().wait_recv()
        make_act(0, theirs)

    @pl.when(has_down)
    def _():
        far_up().wait_recv()
        make_act(rows + 1, theirs)

    @pl.loop(0, rows // 2)
    def _(i):
        c = 2 * i

        @pl.when((i > 0) & (i < rows // 2 - 1))
        def _():
            arrive(c + 1)
            arrive(c + 2)

        found = pair_dot(
            w1, act[pl.ds(c, 3)].reshape(6 * chans, 256), act[pl.ds(c + 1, 3)].reshape(6 * chans, 256)
        )
        for k in range(2):
            a, b = (join_taps(found, chans, 2 * k + f) + emb[...] for f in range(2))
            hid[c + k, :, :128] = a
            hid[c + k, :, 128:] = b
            acc1[...] = acc1[...] + (a + b)
            acc2[...] = acc2[...] + (a * a + b * b)

        found = pair_dot(
            ws, raw[c + 1].reshape(2 * chans, 256), raw[c + 2].reshape(2 * chans, 256)
        )
        skipped[c] = found[:, :256]
        skipped[c + 1] = found[:, 256:]

    per_mid = chans // GROUPS
    stats[2] = pack_sums(acc1[...], acc2[...], per_mid)
    sent_mid = send_all(stats.at[2], slots.at[1], s_send.at[1], s_recv.at[1], peers)
    total = add_all(stats.at[2], slots.at[1], sent_mid)
    mean, rstd = columns_of(total, chans, per_mid, float(entries * per_mid))
    cols_mid[0] = mean
    cols_mid[1] = rstd

    def mid_row(r):
        for f in range(2):
            lanes = pl.ds(f * 128, 128)
            value = silu((hid[r, :, lanes] - cols_mid[0]) * cols_mid[1])
            act2[r + 1, :, lanes] = value.astype(jnp.bfloat16)

    def mid_up():
        return push(act2.at[1], act2.at[rows + 1], m_send.at[1], m_recv.at[1], "strip", strip - 1)

    def mid_down():
        return push(act2.at[rows], act2.at[0], m_send.at[0], m_recv.at[0], "strip", strip + 1)

    mid_row(0)
    pl.when(has_up)(lambda: mid_up().start())
    mid_row(last)
    pl.when(has_down)(lambda: mid_down().start())

    @pl.loop(1, last)
    def _(r):
        mid_row(r)

    has_prev, has_next = frame > 0, frame < n_frame - 1

    def to_prev(c):
        return push(
            tbuf.at[c, 1, :, pl.ds(0, 128)], tbuf.at[c, 2, :, pl.ds(128, 128)],
            t_send.at[0, c], t_recv.at[0, c], "frame", frame - 1,
        )

    def to_next(c):
        return push(
            tbuf.at[c, 1, :, pl.ds(128, 128)], tbuf.at[c, 0, :, pl.ds(0, 128)],
            t_send.at[1, c], t_recv.at[1, c], "frame", frame + 1,
        )

    def inner_first(i):
        tail = i // 2
        return 2 * ((i + 1) * (1 - tail) + (i - 2) * (rows // 2 - 1) * tail)

    @pl.loop(0, rows // 2)
    def _(i):
        first = inner_first(i)

        @pl.when((i == 2) & has_up)
        def _():
            mid_down().wait_recv()

        @pl.when((i == 2) & has_down)
        def _():
            mid_up().wait_recv()

        found = pair_dot(
            w2,
            act2[pl.ds(first, 3)].reshape(3 * chans, 256),
            act2[pl.ds(first + 1, 3)].reshape(3 * chans, 256),
        )
        for k in range(2):
            c = first + k
            for f in range(2):
                lanes = pl.ds(f * 128, 128)
                second = join_taps(found, chans, 2 * k + f)
                hid[c, :, lanes] = second
                inner = silu(second).astype(jnp.bfloat16)
                tbuf[c, 1, :, lanes] = inner
                tbuf[c, 2 * f, :, pl.ds(128 - f * 128, 128)] = inner

            @pl.when(has_prev)
            def _():
                to_prev(c).start()

            @pl.when(has_next)
            def _():
                to_next(c).start()

            @pl.when(frame == 0)
            def _():
                tbuf[c, 0, :, :128] = jnp.zeros((chans, 128), jnp.bfloat16)

            @pl.when(frame == n_frame - 1)
            def _():
                tbuf[c, 2, :, 128:] = jnp.zeros((chans, 128), jnp.bfloat16)

    @pl.loop(0, rows // 2)
    def _(i):
        first = inner_first(i)
        for k in range(2):

            @pl.when(has_prev)
            def _():
                to_next(first + k).wait_recv()

            @pl.when(has_next)
            def _():
                to_prev(first + k).wait_recv()

        mixed = pair_dot(
            wt, tbuf[first].reshape(3 * chans, 256), tbuf[first + 1].reshape(3 * chans, 256)
        )
        for k in range(2):
            c = first + k
            result = mixed[:, 256 * k : 256 * k + 256] + (hid[c] + skipped[c])
            result = result.astype(jnp.bfloat16)
            out[0, c] = result[:, :128]
            out[1, c] = result[:, 128:]

    @pl.loop(0, rows)
    def _(r):
        row_copy(r).wait_send()

        @pl.when(has_prev)
        def _():
            to_prev(r).wait_send()

        @pl.when(has_next)
        def _():
            to_next(r).wait_send()

    for copy in sent + sent_mid:
        copy.wait_send()

    @pl.when(has_up)
    def _():
        own_up().wait_send()
        far_up().wait_send()
        mid_up().wait_send()

    @pl.when(has_down)
    def _():
        own_down().wait_send()
        far_down().wait_send()
        mid_down().wait_send()


def in_kernel(
    enc_feats, skip_feats, timesteps, time_first, time_second, embed_proj,
    conv_first, conv_second, temporal_weight, skip_weight,
):
    own, frames, rows, cols = enc_feats.shape
    chans = conv_second.shape[2]
    width = frames * cols
    temb = time_first.shape[1]
    n_frame, n_strip = lax.axis_size("frame"), lax.axis_size("strip")
    enc, skip = (part.transpose(1, 2, 0, 3) for part in (enc_feats, skip_feats))
    n_peer = n_frame * n_strip - 1
    half_chans = chans // 2
    freq_table = jnp.exp(
        -math.log(10000.0) * jnp.arange(half_chans, dtype=jnp.float32) / half_chans
    )
    angle_rows = timesteps.astype(jnp.float32)[:, None] * freq_table[None, :]
    sinus = jnp.concatenate([jnp.cos(angle_rows), jnp.sin(angle_rows)], axis=1).astype(jnp.bfloat16)
    bf16, f32 = jnp.bfloat16, jnp.float32
    dma = pltpu.SemaphoreType.DMA
    anywhere = pl.BlockSpec(memory_space=pl.ANY)
    inside = pl.BlockSpec(memory_space=pltpu.VMEM)
    pixels = rows * width
    result = pl.pallas_call(
        functools.partial(block_kernel, (n_frame, n_strip)),
        out_shape=jax.ShapeDtypeStruct((frames, rows, chans, cols), bf16),
        in_specs=[anywhere, anywhere, inside] + [anywhere] * 7,
        out_specs=inside,
        scratch_shapes=[
            pltpu.VMEM((rows + 2, 2, chans, width), bf16),
            pltpu.VMEM((rows + 2, 2, chans, width), bf16),
            pltpu.VMEM((rows, chans, width), f32),
            pltpu.VMEM((rows, chans, width), f32),
            pltpu.VMEM((rows + 2, chans, width), bf16),
            pltpu.VMEM((rows, 3, chans, width), bf16),
            pltpu.VMEM((chans, 128), f32),
            pltpu.VMEM((chans, 128), f32),
            pltpu.VMEM((2, 2, chans, 128), f32),
            pltpu.VMEM((2, chans, 128), f32),
            pltpu.VMEM((chans, 128), f32),
            pltpu.VMEM((3 * chans, 6 * chans), bf16),
            pltpu.VMEM((3, 3, chans, chans), bf16),
            pltpu.VMEM((3 * chans, 3 * chans), bf16),
            pltpu.VMEM((3, chans, chans), bf16),
            pltpu.VMEM((chans, 3 * chans), bf16),
            pltpu.VMEM((chans, 2 * chans), bf16),
            pltpu.VMEM((chans, temb), bf16),
            pltpu.VMEM((temb, temb), bf16),
            pltpu.VMEM((chans, temb), bf16),
            pltpu.VMEM((3, 8, 128), f32),
            pltpu.VMEM((2, n_peer, 8, 128), f32),
            pltpu.VMEM((8, 128), f32),
            dma((15,)), dma((2, 2)),
            dma((rows,)), dma((rows,)),
            dma((2,)), dma((2,)), dma((2,)), dma((2,)), dma((2,)), dma((2,)),
            dma((2, rows)), dma((2, rows)),
            dma((2, n_peer)), dma((2, n_peer)),
            dma, dma,
        ],
        compiler_params=pltpu.CompilerParams(
            collective_id=0, has_side_effects=True, vmem_limit_bytes=58 * 2**20
        ),
        cost_estimate=pl.CostEstimate(
            flops=2 * pixels * chans * chans * (18 + 9 + 3 + 2),
            bytes_accessed=14 * 2**20,
            transcendentals=pixels * chans * 4,
        ),
    )(enc, skip, sinus, time_first, time_second, embed_proj.T, conv_first, conv_second, temporal_weight, skip_weight)
    return result.transpose(2, 0, 1, 3)[None]


def block(*args):
    own, frames, rows, cols = args[0].shape
    fits = (
        lax.axis_size("step") == 2
        and own % 16 == 0
        and args[7].shape[2] == 2 * own
        and (own * 4) % GROUPS == 0
        and own % (own * 4 // GROUPS) == 0
        and frames == 2
        and rows == 8
        and cols == 128
    )
    return in_kernel(*args) if fits else on_device(*args)


def solution(mesh):
    return jax.shard_map(
        block,
        mesh=mesh,
        in_specs=(
            P("step", "frame", "strip", None),
            P("step", "frame", "strip", None),
            P("step"),
            P(),
            P(),
            P(),
            P(),
            P(),
            P(),
            P(),
        ),
        out_specs=P("step", None, "frame", "strip", None),
        check_vma=False,
    )
```
